256 devices in a mesh: pipe: 8 (over x_hi, y), expert: 32 (over z, x_lo, core).
Axes of the slice: x: 4 (x_hi: 2, x_lo: 2; x = x_hi * 2 + x_lo), y: 4, z: 8, core: 2. Of those that a mesh axis runs over, the one named last changes fastest.
Arguments:
- grads_sent: bfloat16 [8, 2, 2048, 3584], P('pipe', None, 'expert'), may hold values from -6 to 6
- saved_in: bfloat16 [8, 2, 2048, 3584], P('pipe', None, 'expert'), may hold values from -41 to 41
- routes: int32 [8, 2, 2048, 2], P('pipe', None, 'expert'), may hold values from 0 to 7, as said below
- capacity: int32 [8, 8], P('pipe'), may hold values from 8 to 16, as said below
- saved_pre: bfloat16 [8, 2, 32, 16, 2, 8192], P('pipe', None, None, None, None, 'expert'), may hold values from -6 to 6
- w_gate: bfloat16 [8, 3584, 8192], P('pipe', None, 'expert'), may hold values from -0.09375 to 0.09375
- w_up: bfloat16 [8, 3584, 8192], P('pipe', None, 'expert'), may hold values from -0.09375 to 0.09375
- w_down: bfloat16 [8, 8192, 3584], P('pipe', 'expert'), may hold values from -0.1875 to 0.1875
- router: float32 [8, 3584, 8], P('pipe'), may hold values from -0.09375 to 0.09375
- norm_gain: float32 [8, 3584], P('pipe'), may hold values from 0.25 to 1.75
Outputs:
- grads_in: bfloat16 [8, 2, 2048, 3584], P('pipe', None, 'expert')
The draws below stay inside these ranges and needn't reach their ends.
Inputs may be any that keep to these rules, and one draw needn't show every extreme that they name: `routes`: every row names 2 different experts. In every block of 64 rows that one device holds for one micro-batch, one and the same expert of the section is named by exactly 24 rows, for both micro-batches and all blocks of the section. In every section the expert that all blocks of the section name most often has capacity 16.
All inputs are finite; a program needn't handle non-finite values.
Results may differ from the reference program's by a relative error of at most 0.0061.
Values may be sent and summed in bfloat16 or wider, within the bound.
No kernel may reach another device: no remote copies, remote signals or barrier semaphores. Data moves between devices by JAX's collectives and lax.ppermute only.
A program may use at most 128 MiB of HBM per device.

```python
import math
import jax
import jax.numpy as jnp
from jax import lax

D = 3584
H = 1024
EXPERTS = 8
TOP = 2
T_MB = 64
SECTIONS = 8
TOKENS = 2048
SOURCES = 32
HIDDEN_ALL = 8192
CAP = 16
N_EXPERT = 32


def hot_experts(key):
    return jax.random.randint(jax.random.fold_in(key, 7), (SECTIONS,), 0, EXPERTS)


def block_routes(key, hot_expert):
    key_perm, key_share, key_token, key_turn = jax.random.split(key, 4)
    shuffled = jax.random.permutation(key_perm, EXPERTS)
    ordering = jnp.argsort(jnp.where(shuffled == hot_expert, -1, jnp.arange(EXPERTS)))
    labels = shuffled[ordering]
    others = EXPERTS - 1
    hot_count = CAP + CAP // 2
    shares = jax.random.randint(key_share, (others,), 1, 3)
    remaining = T_MB * TOP - hot_count
    portion = remaining * shares // jnp.sum(shares)
    leftover = remaining - jnp.sum(portion)
    additions = (jnp.arange(others) < leftover).astype(jnp.int32)
    counts = jnp.concatenate([jnp.full((1,), hot_count, jnp.int32), (portion + additions).astype(jnp.int32)])
    boundaries = jnp.cumsum(counts)
    places = jnp.arange(T_MB * TOP)
    ranked = jnp.sum((places[:, None] >= boundaries[None, :]).astype(jnp.int32), axis=1)
    chosen = labels[ranked].reshape(TOP, T_MB).T
    chosen = chosen[jax.random.permutation(key_token, T_MB)]
    offsets = jax.random.randint(key_turn, (T_MB, 1), 0, TOP)
    columns = (jnp.arange(TOP)[None, :] + offsets) % TOP
    return jnp.take_along_axis(chosen, columns, axis=1).astype(jnp.int32)


def draw_routes(key, part):
    hot_expert = hot_experts(key)
    key = jax.random.fold_in(key, 11)
    per_section = 2 * (TOKENS // T_MB)
    block_keys = jax.random.split(key, SECTIONS * per_section)
    hot_block = jnp.repeat(hot_expert, per_section)
    assigned = jax.vmap(block_routes)(block_keys, hot_block)
    return assigned.reshape(SECTIONS, 2, TOKENS, TOP)


def draw_capacity(key, part):
    hot_expert = hot_experts(key)
    key = jax.random.fold_in(key, 13)
    spread_cap = jax.random.randint(key, (SECTIONS, EXPERTS), CAP // 2, CAP + 1)
    return jnp.where(jnp.arange(EXPERTS)[None, :] == hot_expert[:, None], CAP, spread_cap).astype(jnp.int32)


def draw_saved_in(key, part):
    key = jax.random.fold_in(key, 5)
    key_base, key_rows, key_columns = jax.random.split(key, 3)
    entries = jnp.clip(jax.random.normal(key_base, (SECTIONS, 2, TOKENS, D), jnp.float32), -4.5, 4.5)
    row_scale = jnp.exp(jax.random.uniform(key_rows, (SECTIONS, 2, TOKENS, 1), jnp.float32, math.log(0.3), math.log(3.0)))
    column_scale = jnp.exp(jax.random.uniform(key_columns, (D,), jnp.float32, math.log(0.3), math.log(3.0)))
    return (entries * row_scale * column_scale).astype(jnp.bfloat16)


def block_scale(own_key, dims, shards, least, high):
    def one(axis_at, shards_of):
        heights = jax.random.uniform(jax.random.fold_in(jax.random.fold_in(own_key, 6), axis_at), (shards_of,), jnp.float32, least / len(shards), high / len(shards))
        return jnp.repeat(jnp.exp(heights), dims[axis_at] // shards_of).reshape((-1,) + (1,) * (len(dims) - axis_at - 1))

    loudness = one(*shards[0])
    for cut in shards[1:]:
        loudness = loudness * one(*cut)
    return loudness


def noise(own_key, shape, width, most, shards=(), held_as=jnp.bfloat16):
    values = jax.random.normal(own_key, shape, jnp.float32) * width
    if len(shards) > 0:
        values = block_scale(own_key, shape, shards, -0.22, 0.18) * values
    return jnp.clip(values, min=-most, max=most).astype(held_as)


def setup_inputs(seed: int = 0) -> dict:
    keys = jax.random.split(jax.random.key(seed), 11)
    return {
        "grads_sent": noise(keys[0], (SECTIONS, 2, TOKENS, D), 1.0, 6.0, ((0, 8), (2, 32))),
        "saved_in": draw_saved_in(jax.random.fold_in(keys[10], 71), 0),
        "routes": draw_routes(jax.random.fold_in(keys[10], 71), 0),
        "capacity": draw_capacity(jax.random.fold_in(keys[10], 71), 0),
        "saved_pre": noise(keys[4], (SECTIONS, 2, SOURCES, CAP, 2, HIDDEN_ALL), 1.0, 6.0, ((0, 8), (5, 32))),
        "w_gate": noise(keys[5], (SECTIONS, D, HIDDEN_ALL), D ** -0.5, 0.09375, ((0, 8), (2, 32))),
        "w_up": noise(keys[6], (SECTIONS, D, HIDDEN_ALL), D ** -0.5, 0.09375, ((0, 8), (2, 32))),
        "w_down": noise(keys[7], (SECTIONS, HIDDEN_ALL, D), H ** -0.5, 0.1875, ((0, 8), (1, 32))),
        "router": noise(keys[8], (SECTIONS, D, EXPERTS), D ** -0.5, 0.09375, ((0, 8),), jnp.float32),
        "norm_gain": jnp.clip(1.0 + 0.15 * jax.random.normal(keys[9], (SECTIONS, D), jnp.float32), 0.25, 1.75),
    }


ROUTE_SCALE = 2.5
EPSILON = 1e-06
HIGHEST = lax.Precision.HIGHEST

def one_expert(gathered_rows):
    slot_rows, slot_weight, saved_slots, down_weight_matrix, gate_weight_matrix, up_weight_matrix = gathered_rows
    slices = N_EXPERT // EXPERTS
    hidden_dev = H // slices
    projected = jnp.einsum('rd,hd->rh', slot_rows, down_weight_matrix.astype(jnp.float32), precision=HIGHEST)
    gate_pre = saved_slots[:, 0].astype(jnp.float32)
    up_pre = saved_slots[:, 1].astype(jnp.float32)
    gate_sig = jax.nn.sigmoid(gate_pre)
    gate_act = gate_pre * gate_sig
    hidden = gate_act * up_pre
    dw_parts = lax.optimization_barrier(jnp.sum((projected * hidden).reshape(-1, slices, hidden_dev), axis=-1))
    slot_dw = lax.optimization_barrier(jnp.sum(lax.optimization_barrier(dw_parts.astype(jnp.bfloat16)).astype(jnp.float32), axis=-1))
    hidden_grad = slot_weight[:, None] * projected
    gate_grad = (hidden_grad * up_pre * gate_sig * (1.0 + gate_pre * (1.0 - gate_sig))).astype(jnp.bfloat16)
    up_grad = (hidden_grad * gate_act).astype(jnp.bfloat16)
    gate_parts = gate_grad.astype(jnp.float32).reshape(-1, slices, hidden_dev)
    up_parts = up_grad.astype(jnp.float32).reshape(-1, slices, hidden_dev)
    gate_cols = gate_weight_matrix.astype(jnp.float32).reshape(D, slices, hidden_dev)
    up_cols = up_weight_matrix.astype(jnp.float32).reshape(D, slices, hidden_dev)
    partial_value = jnp.einsum('rsh,dsh->rsd', gate_parts, gate_cols, precision=HIGHEST)
    partial_value = partial_value + jnp.einsum('rsh,dsh->rsd', up_parts, up_cols, precision=HIGHEST)
    slot_grad = lax.optimization_barrier(jnp.sum(lax.optimization_barrier(partial_value.astype(jnp.bfloat16)).astype(jnp.float32), axis=1))
    return (slot_grad, slot_dw)

def small_batch_gradient(incoming_batches, input_rows, selected_expert_index, expert_limits, stored_activations, gate_weight_matrix, up_weight_matrix, down_weight_matrix, router_weight_matrix, norm_gain_row):
    slot_total = EXPERTS * SOURCES * CAP
    values = input_rows.astype(jnp.float32)
    inv_rms = lax.rsqrt(lax.optimization_barrier(jnp.mean(values * values, axis=-1, keepdims=True)) + EPSILON)
    normed = values * inv_rms * norm_gain_row
    scores = jax.nn.sigmoid(jnp.dot(normed, router_weight_matrix, precision=HIGHEST))
    picked = selected_expert_index[:, :, None] == jnp.arange(EXPERTS, dtype=jnp.int32)[None, None, :]
    picked_mask = picked.astype(jnp.float32)
    chosen = lax.optimization_barrier(jnp.sum(picked_mask * scores[:, None, :], axis=-1))
    totals = lax.optimization_barrier(jnp.sum(chosen, axis=-1, keepdims=True))
    weights = ROUTE_SCALE * chosen / totals
    counts = lax.optimization_barrier(jnp.sum(picked.astype(jnp.int32), axis=1)).reshape(SOURCES, T_MB, EXPERTS)
    before = (jnp.cumsum(counts, axis=1) - counts).reshape(TOKENS, EXPERTS)
    slot_positions = jnp.take_along_axis(before, selected_expert_index, axis=1)
    retain_mask = slot_positions < jnp.take(expert_limits, selected_expert_index)
    source_index = (jnp.arange(TOKENS, dtype=jnp.int32) // T_MB)[:, None]
    flat_index = jnp.where(retain_mask, (selected_expert_index * SOURCES + source_index) * CAP + slot_positions, slot_total).astype(jnp.int32)
    flat_list = flat_index.reshape(-1)
    sent_weight = lax.optimization_barrier(weights.astype(jnp.bfloat16)).astype(jnp.float32)
    slot_rows = jnp.zeros((slot_total, D), jnp.float32).at[flat_list].add(jnp.repeat(incoming_batches.astype(jnp.float32), TOP, axis=0), mode='drop')
    slot_weight = jnp.zeros((slot_total,), jnp.float32).at[flat_list].add(sent_weight.reshape(-1), mode='drop')
    saved_slots = jnp.transpose(stored_activations.reshape(SOURCES, CAP, 2, EXPERTS, H), (3, 0, 1, 2, 4)).reshape(EXPERTS, SOURCES * CAP, 2, H)
    downs = down_weight_matrix.reshape(EXPERTS, H, D)
    gates = jnp.transpose(gate_weight_matrix.reshape(D, EXPERTS, H), (1, 0, 2))
    ups = jnp.transpose(up_weight_matrix.reshape(D, EXPERTS, H), (1, 0, 2))
    slot_grad, slot_dw = lax.map(one_expert, (slot_rows.reshape(EXPERTS, SOURCES * CAP, D), slot_weight.reshape(EXPERTS, SOURCES * CAP), saved_slots, downs, gates, ups))
    padded_grad = jnp.concatenate([slot_grad.reshape(slot_total, D), jnp.zeros((1, D), jnp.float32)], axis=0)
    padded_dw = jnp.concatenate([slot_dw.reshape(slot_total), jnp.zeros((1,), jnp.float32)], axis=0)
    expert_grad = lax.optimization_barrier(jnp.sum(jnp.take(padded_grad, flat_index, axis=0), axis=1))
    choice_dw = jnp.take(padded_dw, flat_index, axis=0)
    chosen_grad = ROUTE_SCALE * (choice_dw / totals - lax.optimization_barrier(jnp.sum(choice_dw * chosen, axis=-1, keepdims=True)) / (totals * totals))
    score_grad = lax.optimization_barrier(jnp.sum(picked_mask * chosen_grad[:, :, None], axis=1)) * scores * (1.0 - scores)
    normed_grad = expert_grad + jnp.dot(score_grad, router_weight_matrix.T, precision=HIGHEST)
    scaled = norm_gain_row * normed_grad
    result = incoming_batches.astype(jnp.float32) + inv_rms * scaled - inv_rms * inv_rms * inv_rms * values * lax.optimization_barrier(jnp.mean(values * scaled, axis=-1, keepdims=True))
    return result.astype(jnp.bfloat16)

def reference(grads_sent, saved_in, routes, capacity, saved_pre, w_gate, w_up, w_down, router, norm_gain):
    incoming = jnp.stack([jnp.roll(grads_sent[:, 0], -1, axis=0), jnp.roll(grads_sent[:, 1], 1, axis=0)], axis=1)

    def section_grad(gathered_rows):
        incoming_batches, input_rows, selected_expert_index, expert_limits, stored_activations, gate_weight_matrix, up_weight_matrix, down_weight_matrix, router_weight_matrix, norm_gain_row = gathered_rows
        section_outputs = [small_batch_gradient(incoming_batches[membership_mask], input_rows[membership_mask], selected_expert_index[membership_mask], expert_limits, stored_activations[membership_mask], gate_weight_matrix, up_weight_matrix, down_weight_matrix, router_weight_matrix, norm_gain_row) for membership_mask in range(2)]
        return jnp.stack(section_outputs, axis=0)
    return lax.map(section_grad, (incoming, saved_in, routes, capacity, saved_pre, w_gate, w_up, w_down, router, norm_gain))
```

```python
import functools

import jax
import jax.numpy as jnp
from jax import lax
from jax.experimental import pallas as pl
from jax.experimental.pallas import tpu as pltpu
from jax.sharding import PartitionSpec as P

ROUTE_SCALE = 2.5
EPSILON = 1e-06
HIGHEST = lax.Precision.HIGHEST
F32 = jnp.float32
BF16 = jnp.bfloat16
D = 3584
EXPERTS = 8
CAP = 16
TOKENS = 64
SLOTS = EXPERTS * CAP
SLICE = 256
WIDE = D + 128
UNIT = 2 * CAP
NT = (((1,), (1,)), ((), ()))
TN = (((0,), (0,)), ((), ()))
GROUPS = ((0,), (1, 7), (2, 6), (3, 5), (4,))

VMEM = pl.BlockSpec(memory_space=pltpu.VMEM)
SMEM = pl.BlockSpec(memory_space=pltpu.SMEM)


def pipe_shift(value, by):
    return lax.ppermute(value, "pipe", [(i, (i + by) % 8) for i in range(8)])


def z_shift(value, by):
    pairs = [(i, ((i // 4 + by) % 8) * 4 + i % 4) for i in range(32)]
    return lax.ppermute(value, "expert", pairs)


def x_swap(value):
    return lax.ppermute(value, "expert", [(i, i ^ 2) for i in range(32)])


def core_swap(value):
    return lax.ppermute(value, "expert", [(i, i ^ 1) for i in range(32)])


def call(kernel, outs, specs, flops, moved):
    return pl.pallas_call(
        kernel,
        out_shape=outs,
        in_specs=specs,
        out_specs=jax.tree.map(lambda _: VMEM, outs),
        cost_estimate=pl.CostEstimate(flops=flops, bytes_accessed=moved, transcendentals=0),
        compiler_params=pltpu.CompilerParams(vmem_limit_bytes=40 * 1024 * 1024),
    )


def lanes(value_hi, value_lo, shape):
    lane = lax.broadcasted_iota(jnp.int32, shape, 1)
    return jnp.where(lane == 0, value_hi, jnp.where(lane == 1, value_lo, 0.0))


def split_sum(tile):
    total = jnp.sum(tile, axis=-1, keepdims=True)
    high = total.astype(BF16).astype(F32)
    return high, total - high


def prep_kernel(place, limits, routes, saved, gain, router, match, weight, scores, inv):
    z = place[0]
    slot = lax.broadcasted_iota(jnp.int32, (SLOTS, TOKENS), 0)
    expert = ((slot >> 4) + z) & (EXPERTS - 1)
    number = slot & (CAP - 1)
    limit = jnp.zeros((SLOTS, TOKENS), jnp.int32)
    for e in range(EXPERTS):
        limit = jnp.where(expert == e, limits[e], limit)
    allowed = number < limit
    earlier = (
        lax.broadcasted_iota(jnp.int32, (TOKENS, TOKENS), 0)
        < lax.broadcasted_iota(jnp.int32, (TOKENS, TOKENS), 1)
    ).astype(BF16)
    names = lax.broadcasted_iota(jnp.int32, (EXPERTS, TOKENS), 0)
    for m in range(2):
        values = saved[m].astype(F32)
        inv_rms = lax.rsqrt(jnp.mean(values * values, axis=-1, keepdims=True) + EPSILON)
        inv[m] = inv_rms
        normed = values * inv_rms * gain[...]
        logits = lax.dot_general(
            router[...], normed, NT, precision=HIGHEST, preferred_element_type=F32
        )
        score = jax.nn.sigmoid(logits)
        scores[m] = score
        picked = [routes[m, k : k + 1, :] == expert for k in range(2)]
        chosen = [
            jnp.sum(jnp.where(routes[m, k : k + 1, :] == names, score, 0.0), axis=0, keepdims=True)
            for k in range(2)
        ]
        totals = chosen[0] + chosen[1]
        counts = picked[0].astype(F32) + picked[1].astype(F32)
        before = jnp.dot(counts.astype(BF16), earlier, preferred_element_type=F32)
        kept = allowed & (before.astype(jnp.int32) == number)
        column = jnp.zeros((SLOTS, 1), F32)
        for k in range(2):
            hit = (picked[k] & kept).astype(F32)
            match[m, k] = hit
            share = (ROUTE_SCALE * chosen[k] / totals).astype(BF16).astype(F32)
            column = column + jnp.sum(hit * share, axis=-1, keepdims=True)
        weight[m] = jnp.broadcast_to(column, (SLOTS, 128)).astype(BF16)


def spread_kernel(first, second, match, weight, *outs):
    for m, rows in enumerate((first, second)):
        both = (match[m, 0] + match[m, 1]).astype(BF16)
        filled = jnp.dot(both, rows[...], preferred_element_type=F32).astype(BF16)
        for k in range(EXPERTS):
            outs[k][m * CAP : (m + 1) * CAP, :D] = filled[k * CAP : (k + 1) * CAP]
            outs[k][m * CAP : (m + 1) * CAP, D:] = weight[m, k * CAP : (k + 1) * CAP]


def unit_kernel(shifts, place, *refs):
    n = len(shifts)
    units = refs[: 2 * n]
    pre_own, pre_other = refs[2 * n : 2 * n + 2]
    downs = refs[2 * n + 2 : 2 * n + 4]
    gates = refs[2 * n + 4 : 2 * n + 6]
    ups = refs[2 * n + 6 : 2 * n + 8]
    own, away, rows = refs[2 * n + 8 :]
    z, x = place[0], place[1]
    size = UNIT * 2 * n
    for i in range(2 * n):
        rows[i * UNIT : (i + 1) * UNIT] = units[i][...]
    weight = rows[:, D:].astype(F32)[:, :1]
    total = jnp.zeros((size, 1), F32)
    gate_grads, up_grads = [], []
    for saved, down in ((pre_own, downs[0]), (pre_other, downs[1])):
        projected = lax.dot_general(rows[:, :D], down[...], NT, preferred_element_type=F32)
        parts = [[], []]
        for side in range(2):
            for i in range(n):
                source = (z + 8 - shifts[i]) & 7
                column = x if side == 0 else 1 - x
                for part in range(2):
                    parts[part].append(saved[source, column, part].reshape(UNIT, SLICE))
        gate = jnp.concatenate(parts[0], axis=0).astype(F32)
        up = jnp.concatenate(parts[1], axis=0).astype(F32)
        sig = jax.nn.sigmoid(gate)
        act = gate * sig
        total = total + jnp.sum(projected * (act * up), axis=-1, keepdims=True)
        grad = weight * projected
        gate_grads.append((grad * up * sig * (1.0 + gate * (1.0 - sig))).astype(BF16))
        up_grads.append((grad * act).astype(BF16))
    half = size // 2
    step = 512
    for at in range(0, D, step):
        part = jnp.zeros((size, step), F32)
        for s in range(2):
            part = part + lax.dot_general(
                gate_grads[s], gates[s][at : at + step], NT, preferred_element_type=F32
            )
            part = part + lax.dot_general(
                up_grads[s], ups[s][at : at + step], NT, preferred_element_type=F32
            )
        own[:, at : at + step] = part[:half]
        away[:, at : at + step] = part[half:].astype(BF16)
    high, low = split_sum(total)
    tile = lanes(high, low, (size, 128))
    own[:, D:] = tile[:half]
    away[:, D:] = tile[half:].astype(BF16)


def add_kernel(own, got, *outs):
    for i, out in enumerate(outs):
        at = slice(i * UNIT, (i + 1) * UNIT)
        out[:, :D] = (own[at, :D] + got[at, :D].astype(F32)).astype(BF16)
        high, low = split_sum(own[at, D:] + got[at, D:].astype(F32))
        out[:, D:] = lanes(high, low, (UNIT, 128)).astype(BF16)


def finish_kernel(
    own, got, b1, b2, b3, b4, b5, b6, b7, first, second, saved, routes, match, scores, inv,
    gain, router, out, back,
):
    units = (None, b1, b2, b3, b4, b5, b6, b7)
    names = lax.broadcasted_iota(jnp.int32, (EXPERTS, TOKENS), 0)
    for m, incoming in enumerate((first, second)):
        at = slice(m * CAP, (m + 1) * CAP)
        back[:CAP] = (own[at, :D] + got[at, :D].astype(F32)).astype(BF16)
        dws = [own[at, D:] + got[at, D:].astype(F32)]
        for k in range(1, EXPERTS):
            back[k * CAP : (k + 1) * CAP] = units[k][at, :D]
            dws.append(units[k][at, D:].astype(F32))
        slot_dw = jnp.sum(jnp.concatenate(dws, axis=0), axis=-1, keepdims=True)
        score = scores[m]
        chosen, choice = [], []
        for k in range(2):
            mine = routes[m, k : k + 1, :] == names
            chosen.append(jnp.sum(jnp.where(mine, score, 0.0), axis=0, keepdims=True))
            choice.append(jnp.sum(match[m, k] * slot_dw, axis=0, keepdims=True))
        totals = chosen[0] + chosen[1]
        inner = (choice[0] * chosen[0] + choice[1] * chosen[1]) / (totals * totals)
        score_grad = jnp.zeros((EXPERTS, TOKENS), F32)
        for k in range(2):
            mine = routes[m, k : k + 1, :] == names
            slope = ROUTE_SCALE * (choice[k] / totals - inner)
            score_grad = score_grad + jnp.where(mine, slope, 0.0)
        score_grad = score_grad * score * (1.0 - score)
        both = (match[m, 0] + match[m, 1]).astype(BF16)
        total = lax.dot_general(both, back[...], TN, preferred_element_type=F32)
        total = total + lax.dot_general(
            score_grad, router[...], TN, precision=HIGHEST, preferred_element_type=F32
        )
        scaled = gain[...] * total
        values = saved[m].astype(F32)
        inv_rms = inv[m]
        mean = jnp.mean(values * scaled, axis=-1, keepdims=True)
        out[m] = (
            incoming[...].astype(F32)
            + inv_rms * scaled
            - (inv_rms * inv_rms * inv_rms * mean) * values
        ).astype(BF16)


def shape(dims, dtype=BF16):
    return jax.ShapeDtypeStruct(dims, dtype)


def local(
    grads_sent, saved_in, routes, capacity, saved_pre, w_gate, w_up, w_down, router, norm_gain
):
    index = lax.axis_index("expert")
    core = index % 2
    place = jnp.stack([index // 4, (index // 2) % 2]).astype(jnp.int32)
    first = pipe_shift(grads_sent[0, 0], -1)
    second = pipe_shift(grads_sent[0, 1], 1)
    downs = (w_down[0], core_swap(w_down[0]))
    gates = (w_gate[0], core_swap(w_gate[0]))
    ups = (w_up[0], core_swap(w_up[0]))
    pre = saved_pre[0].reshape(2, 8, 2, 2, CAP, 2, SLICE)
    pre = jnp.transpose(pre, (3, 1, 2, 5, 0, 4, 6))
    pre_own = lax.dynamic_index_in_dim(pre, core, 0, keepdims=False)
    pre_other = core_swap(lax.dynamic_index_in_dim(pre, 1 - core, 0, keepdims=False))
    routes_t = jnp.transpose(routes[0], (0, 2, 1))
    router_t = router[0].T
    match, weight, scores, inv = call(
        prep_kernel,
        (
            shape((2, 2, SLOTS, TOKENS), F32),
            shape((2, SLOTS, 128)),
            shape((2, EXPERTS, TOKENS), F32),
            shape((2, TOKENS, 1), F32),
        ),
        [SMEM, SMEM] + [VMEM] * 4,
        500_000_000,
        3_000_000,
    )(place, capacity[0], routes_t, saved_in[0], norm_gain, router_t)
    units = call(
        spread_kernel,
        tuple(shape((UNIT, WIDE)) for _ in range(EXPERTS)),
        [VMEM] * 4,
        500_000_000,
        4_000_000,
    )(first, second, match, weight)
    mine = [units[0]] + [z_shift(units[k], k) for k in range(1, EXPERTS)]
    theirs = [x_swap(unit) for unit in mine]
    back = [None] * EXPERTS
    for group in GROUPS:
        n = len(group)
        own, away = pl.pallas_call(
            functools.partial(unit_kernel, group),
            out_shape=(shape((UNIT * n, WIDE), F32), shape((UNIT * n, WIDE))),
            in_specs=[SMEM] + [VMEM] * (2 * n + 8),
            out_specs=(VMEM, VMEM),
            scratch_shapes=[pltpu.VMEM((2 * UNIT * n, WIDE), BF16)],
            cost_estimate=pl.CostEstimate(
                flops=3_000_000_000, bytes_accessed=12_000_000, transcendentals=0
            ),
            compiler_params=pltpu.CompilerParams(vmem_limit_bytes=40 * 1024 * 1024),
        )(
            place,
            *[mine[k] for k in group],
            *[theirs[k] for k in group],
            pre_own,
            pre_other,
            *downs,
            *gates,
            *ups,
        )
        got = x_swap(away)
        if group == (0,):
            back[0] = (own, got)
            continue
        sums = call(
            add_kernel,
            tuple(shape((UNIT, WIDE)) for _ in group),
            [VMEM] * 2,
            10_000_000,
            2_000_000,
        )(own, got)
        for k, value in zip(group, sums):
            back[k] = z_shift(value, -k)
    out = pl.pallas_call(
        finish_kernel,
        out_shape=shape((2, TOKENS, D)),
        in_specs=[VMEM] * 18,
        out_specs=VMEM,
        scratch_shapes=[pltpu.VMEM((SLOTS, D), BF16)],
        cost_estimate=pl.CostEstimate(
            flops=500_000_000, bytes_accessed=6_000_000, transcendentals=0
        ),
        compiler_params=pltpu.CompilerParams(vmem_limit_bytes=40 * 1024 * 1024),
    )(
        *back[0],
        *back[1:],
        first,
        second,
        saved_in[0],
        routes_t,
        match,
        scores,
        inv,
        norm_gain,
        router_t,
    )
    return out[None]


def solution(mesh):
    return jax.shard_map(
        local,
        mesh=mesh,
        in_specs=(
            P("pipe", None, "expert", None),
            P("pipe", None, "expert", None),
            P("pipe", None, "expert", None),
            P("pipe", None),
            P("pipe", None, None, None, None, "expert"),
            P("pipe", None, "expert"),
            P("pipe", None, "expert"),
            P("pipe", "expert", None),
            P("pipe", None, None),
            P("pipe", None),
        ),
        out_specs=P("pipe", None, "expert", None),
        check_vma=False,
    )
```

```python
import functools

import jax
import jax.numpy as jnp
from jax import lax
from jax.experimental import pallas as pl
from jax.experimental.pallas import tpu as pltpu
from jax.sharding import PartitionSpec as P

ROUTE_SCALE = 2.5
EPSILON = 1e-06
HIGHEST = lax.Precision.HIGHEST
F32 = jnp.float32
BF16 = jnp.bfloat16
D = 3584
EXPERTS = 8
CAP = 16
TOKENS = 64
SLOTS = EXPERTS * CAP
SLICE = 256
WIDE = D + 128
UNIT = 2 * CAP
NT = (((1,), (1,)), ((), ()))
TN = (((0,), (0,)), ((), ()))
COST = 100_000
WORK = 2_000_000_000
LIMIT = 24 * 1024 * 1024

VMEM = pl.BlockSpec(memory_space=pltpu.VMEM)
SMEM = pl.BlockSpec(memory_space=pltpu.SMEM)


def pipe_shift(value, by):
    return lax.ppermute(value, "pipe", [(i, (i + by) % 8) for i in range(8)])


def z_shift(value, by):
    pairs = [(i, ((i // 4 + by) % 8) * 4 + i % 4) for i in range(32)]
    return lax.ppermute(value, "expert", pairs)


def x_swap(value):
    return lax.ppermute(value, "expert", [(i, i ^ 2) for i in range(32)])


def core_swap(value):
    return lax.ppermute(value, "expert", [(i, i ^ 1) for i in range(32)])


def call(kernel, outs, specs, flops, moved):
    return pl.pallas_call(
        kernel,
        out_shape=outs,
        in_specs=specs,
        out_specs=jax.tree.map(lambda _: VMEM, outs),
        cost_estimate=pl.CostEstimate(flops=flops, bytes_accessed=moved, transcendentals=0),
        compiler_params=pltpu.CompilerParams(vmem_limit_bytes=LIMIT),
    )


def lanes(value_hi, value_lo, shape):
    lane = lax.broadcasted_iota(jnp.int32, shape, 1)
    return jnp.where(lane == 0, value_hi, jnp.where(lane == 1, value_lo, 0.0))


def split_sum(tile):
    total = jnp.sum(tile, axis=-1, keepdims=True)
    high = total.astype(BF16).astype(F32)
    return high, total - high


def prep_kernel(place, limits, routes, saved, gain, router, match, weight, scores, inv):
    z = place[0]
    slot = lax.broadcasted_iota(jnp.int32, (SLOTS, TOKENS), 0)
    expert = ((slot >> 4) + z) & (EXPERTS - 1)
    number = slot & (CAP - 1)
    limit = jnp.zeros((SLOTS, TOKENS), jnp.int32)
    for e in range(EXPERTS):
        limit = jnp.where(expert == e, limits[e], limit)
    allowed = number < limit
    earlier = (
        lax.broadcasted_iota(jnp.int32, (TOKENS, TOKENS), 0)
        < lax.broadcasted_iota(jnp.int32, (TOKENS, TOKENS), 1)
    ).astype(BF16)
    names = lax.broadcasted_iota(jnp.int32, (EXPERTS, TOKENS), 0)
    for m in range(2):
        values = saved[m].astype(F32)
        inv_rms = lax.rsqrt(jnp.mean(values * values, axis=-1, keepdims=True) + EPSILON)
        inv[m] = inv_rms
        normed = values * inv_rms * gain[...]
        logits = lax.dot_general(
            router[...], normed, NT, precision=HIGHEST, preferred_element_type=F32
        )
        score = jax.nn.sigmoid(logits)
        scores[m] = score
        picked = [routes[m, k : k + 1, :] == expert for k in range(2)]
        chosen = [
            jnp.sum(jnp.where(routes[m, k : k + 1, :] == names, score, 0.0), axis=0, keepdims=True)
            for k in range(2)
        ]
        totals = chosen[0] + chosen[1]
        counts = picked[0].astype(F32) + picked[1].astype(F32)
        before = jnp.dot(counts.astype(BF16), earlier, preferred_element_type=F32)
        kept = allowed & (before.astype(jnp.int32) == number)
        column = jnp.zeros((SLOTS, 1), F32)
        for k in range(2):
            hit = (picked[k] & kept).astype(F32)
            match[m, k] = hit
            share = (ROUTE_SCALE * chosen[k] / totals).astype(BF16).astype(F32)
            column = column + jnp.sum(hit * share, axis=-1, keepdims=True)
        weight[m] = jnp.broadcast_to(column, (SLOTS, 128)).astype(BF16)


def spread_kernel(first, second, match, weight, kept, *outs):
    for m, rows in enumerate((first, second)):
        kept[m] = rows[...]
        both = (match[m, 0] + match[m, 1]).astype(BF16)
        filled = jnp.dot(both, rows[...], preferred_element_type=F32).astype(BF16)
        for k in range(EXPERTS):
            outs[k][m * CAP : (m + 1) * CAP, :D] = filled[k * CAP : (k + 1) * CAP]
            outs[k][m * CAP : (m + 1) * CAP, D:] = weight[m, k * CAP : (k + 1) * CAP]


def stage_kernel(w_down, w_gate, w_up, packed):
    step = 512
    packed[:SLICE] = w_down[0]
    for at in range(0, D, step):
        packed[SLICE : 2 * SLICE, at : at + step] = w_gate[0, at : at + step].T
        packed[2 * SLICE :, at : at + step] = w_up[0, at : at + step].T


def pack_kernel(low, high, out):
    out[:UNIT] = low[...]
    out[UNIT:] = high[...]


def unit_kernel(shifts, place, mine, theirs, *refs):
    saved, weights = refs[0:2], refs[2:4]
    own, away, rows = refs[4:]
    n = len(shifts)
    z, x = place[0], place[1]
    size = UNIT * 2 * n
    half = size // 2
    rows[:half] = mine[...]
    rows[half:] = theirs[...]
    weight = rows[:, D:].astype(F32)[:, :1]
    total = jnp.zeros((size, 1), F32)
    grads = []
    for s in range(2):
        parts = [[], []]
        for side in range(2):
            for shift in shifts:
                source = (z + 8 - shift) & 7
                column = x if side == 0 else 1 - x
                for part in range(2):
                    parts[part].append(saved[s][source, column, part].reshape(UNIT, SLICE))
        gate = jnp.concatenate(parts[0], axis=0).astype(F32)
        up = jnp.concatenate(parts[1], axis=0).astype(F32)
        projected = lax.dot_general(
            rows[:, :D], weights[s][:SLICE], NT, preferred_element_type=F32
        )
        sig = jax.nn.sigmoid(gate)
        act = gate * sig
        total = total + jnp.sum(projected * (act * up), axis=-1, keepdims=True)
        grad = weight * projected
        gate_grad = (grad * up * sig * (1.0 + gate * (1.0 - sig))).astype(BF16)
        grads.append(jnp.concatenate([gate_grad, (grad * act).astype(BF16)], axis=1))
    step = 512
    for at in range(0, D, step):
        part = jnp.dot(grads[0], weights[0][SLICE:, at : at + step], preferred_element_type=F32)
        part = part + jnp.dot(
            grads[1], weights[1][SLICE:, at : at + step], preferred_element_type=F32
        )
        own[:, at : at + step] = part[:half]
        away[:, at : at + step] = part[half:].astype(BF16)
    high, low = split_sum(total)
    tile = lanes(high, low, (size, 128))
    own[:, D:] = tile[:half]
    away[:, D:] = tile[half:].astype(BF16)


def add_kernel(own, got, *outs):
    for i, out in enumerate(outs):
        at = slice(i * UNIT, (i + 1) * UNIT)
        out[:, :D] = (own[at, :D] + got[at, :D].astype(F32)).astype(BF16)
        high, low = split_sum(own[at, D:] + got[at, D:].astype(F32))
        out[:, D:] = lanes(high, low, (UNIT, 128)).astype(BF16)


def finish_kernel(
    own, got, b1, b2, b3, b4, b5, b6, b7, kept, saved, routes, match, scores, inv,
    gain, router, out, back,
):
    units = (None, b1, b2, b3, b4, b5, b6, b7)
    names = lax.broadcasted_iota(jnp.int32, (EXPERTS, TOKENS), 0)
    for m in range(2):
        at = slice(m * CAP, (m + 1) * CAP)
        back[:CAP] = (own[at, :D] + got[at, :D].astype(F32)).astype(BF16)
        dws = [own[at, D:] + got[at, D:].astype(F32)]
        for k in range(1, EXPERTS):
            back[k * CAP : (k + 1) * CAP] = units[k][at, :D]
            dws.append(units[k][at, D:].astype(F32))
        slot_dw = jnp.sum(jnp.concatenate(dws, axis=0), axis=-1, keepdims=True)
        score = scores[m]
        chosen, choice = [], []
        for k in range(2):
            mine = routes[m, k : k + 1, :] == names
            chosen.append(jnp.sum(jnp.where(mine, score, 0.0), axis=0, keepdims=True))
            choice.append(jnp.sum(match[m, k] * slot_dw, axis=0, keepdims=True))
        totals = chosen[0] + chosen[1]
        inner = (choice[0] * chosen[0] + choice[1] * chosen[1]) / (totals * totals)
        score_grad = jnp.zeros((EXPERTS, TOKENS), F32)
        for k in range(2):
            mine = routes[m, k : k + 1, :] == names
            slope = ROUTE_SCALE * (choice[k] / totals - inner)
            score_grad = score_grad + jnp.where(mine, slope, 0.0)
        score_grad = score_grad * score * (1.0 - score)
        both = (match[m, 0] + match[m, 1]).astype(BF16)
        total = lax.dot_general(both, back[...], TN, preferred_element_type=F32)
        total = total + lax.dot_general(
            score_grad, router[...], TN, precision=HIGHEST, preferred_element_type=F32
        )
        scaled = gain[...] * total
        values = saved[m].astype(F32)
        inv_rms = inv[m]
        mean = jnp.mean(values * scaled, axis=-1, keepdims=True)
        out[m] = (
            kept[m].astype(F32)
            + inv_rms * scaled
            - (inv_rms * inv_rms * inv_rms * mean) * values
        ).astype(BF16)


def shape(dims, dtype=BF16):
    return jax.ShapeDtypeStruct(dims, dtype)


def local(
    grads_sent, saved_in, routes, capacity, saved_pre, w_gate, w_up, w_down, router, norm_gain
):
    index = lax.axis_index("expert")
    core = index % 2
    place = jnp.stack([index // 4, (index // 2) % 2]).astype(jnp.int32)
    first, second = lax.optimization_barrier((grads_sent[0, 0], grads_sent[0, 1]))
    first, second = pipe_shift(first, -1), pipe_shift(second, 1)
    packed = call(stage_kernel, shape((3 * SLICE, D)), [VMEM] * 3, COST, 1000)(
        w_down, w_gate, w_up
    )
    pre = saved_pre[0].reshape(2, 8, 2, 2, CAP, 2, SLICE)
    pre = jnp.transpose(pre, (3, 1, 2, 5, 0, 4, 6))
    routes_t = jnp.transpose(routes[0], (0, 2, 1))
    router_t = router[0].T
    match, weight, scores, inv = call(
        prep_kernel,
        (
            shape((2, 2, SLOTS, TOKENS), F32),
            shape((2, SLOTS, 128)),
            shape((2, EXPERTS, TOKENS), F32),
            shape((2, TOKENS, 1), F32),
        ),
        [SMEM, SMEM] + [VMEM] * 4,
        COST,
        1000,
    )(place, capacity[0], routes_t, saved_in[0], norm_gain, router_t)
    pre_own = lax.dynamic_index_in_dim(pre, core, 0, keepdims=False)
    pre_other = lax.dynamic_index_in_dim(pre, 1 - core, 0, keepdims=False)
    first, second, packed, pre_own, pre_other, weight = lax.optimization_barrier(
        (first, second, packed, pre_own, pre_other, weight)
    )
    pre_other, weights = core_swap(pre_other), (packed, core_swap(packed))
    kept, *units = call(
        spread_kernel,
        (shape((2, TOKENS, D)),) + tuple(shape((UNIT, WIDE)) for _ in range(EXPERTS)),
        [VMEM] * 4,
        COST,
        1000,
    )(first, second, match, weight)
    def work(group, mine, theirs):
        n = len(group)
        return pl.pallas_call(
            functools.partial(unit_kernel, group),
            out_shape=(shape((UNIT * n, WIDE), F32), shape((UNIT * n, WIDE))),
            in_specs=[SMEM] + [VMEM] * 6,
            out_specs=(VMEM, VMEM),
            scratch_shapes=[pltpu.VMEM((2 * UNIT * n, WIDE), BF16)],
            cost_estimate=pl.CostEstimate(flops=WORK, bytes_accessed=1000, transcendentals=0),
            compiler_params=pltpu.CompilerParams(vmem_limit_bytes=LIMIT),
        )(place, mine, theirs, pre_own, pre_other, *weights)

    def add(group, own, got):
        return call(add_kernel, tuple(shape((UNIT, WIDE)) for _ in group), [VMEM] * 2, COST, 1000)(
            own, got
        )

    def pack(low, high):
        return call(pack_kernel, shape((2 * UNIT, WIDE)), [VMEM] * 2, COST, 1000)(low, high)

    v = {"u%d" % k: units[k] for k in range(EXPERTS)}

    def tie(names):
        names = names.split()
        v.update(zip(names, lax.optimization_barrier(tuple(v[n] for n in names))))

    def z_out(*shifts):
        for k in shifts:
            v["m%d" % k] = z_shift(v["u%d" % k], k)

    def z_back(*shifts):
        for k in shifts:
            v["b%d" % k] = z_shift(v["d%d" % k], -k)

    v["t0"] = x_swap(v["u0"])
    z_out(1, 7)
    tie("t0 u0 m1 m7 u3 u5")
    z_out(3, 5)
    v["p1"] = pack(v["m1"], v["m7"])
    v["t1"] = x_swap(v["p1"])
    v["own1"], v["away1"] = work((1, 7), v["p1"], v["t1"])
    tie("m3 m5 own1 away1 u2 u6 u4 t0 u0")
    z_out(4, 2, 6)
    v["p3"] = pack(v["m3"], v["m5"])
    v["t3"] = x_swap(v["p3"])
    v["got1"] = x_swap(v["away1"])
    v["own3"], v["away3"] = work((3, 5), v["p3"], v["t3"])
    tie("got1 own1 own3 away3 m4 m2 m6 t0 u0")
    v["d1"], v["d7"] = add((1, 7), v["own1"], v["got1"])
    z_back(1, 7)
    v["t4"] = x_swap(v["m4"])
    v["got3"] = x_swap(v["away3"])
    v["own4"], v["away4"] = work((4,), v["m4"], v["t4"])
    tie("b1 b7 own4 away4 got3 own3 m2 m6 t0 u0")
    v["d3"], v["d5"] = add((3, 5), v["own3"], v["got3"])
    z_back(3, 5)
    v["p2"] = pack(v["m2"], v["m6"])
    v["t2"] = x_swap(v["p2"])
    v["got4"] = x_swap(v["away4"])
    v["own2"], v["away2"] = work((2, 6), v["p2"], v["t2"])
    tie("b3 b5 own2 away2 got4 own4 t0 u0")
    (v["d4"],) = add((4,), v["own4"], v["got4"])
    z_back(4)
    v["got2"] = x_swap(v["away2"])
    v["own0"], v["away0"] = work((0,), v["u0"], v["t0"])
    tie("b4 got2 own2 own0 away0")
    v["got0"] = x_swap(v["away0"])
    v["d2"], v["d6"] = add((2, 6), v["own2"], v["got2"])
    z_back(2, 6)
    back = [(v["own0"], v["got0"])] + [v["b%d" % k] for k in range(1, EXPERTS)]
    out = pl.pallas_call(
        finish_kernel,
        out_shape=shape((2, TOKENS, D)),
        in_specs=[VMEM] * 17,
        out_specs=VMEM,
        scratch_shapes=[pltpu.VMEM((SLOTS, D), BF16)],
        cost_estimate=pl.CostEstimate(
            flops=COST, bytes_accessed=1000, transcendentals=0
        ),
        compiler_params=pltpu.CompilerParams(vmem_limit_bytes=LIMIT),
    )(
        *back[0],
        *back[1:],
        kept,
        saved_in[0],
        routes_t,
        match,
        scores,
        inv,
        norm_gain,
        router_t,
    )
    return out[None]


def solution(mesh):
    return jax.shard_map(
        local,
        mesh=mesh,
        in_specs=(
            P("pipe", None, "expert", None),
            P("pipe", None, "expert", None),
            P("pipe", None, "expert", None),
            P("pipe", None),
            P("pipe", None, None, None, None, "expert"),
            P("pipe", None, "expert"),
            P("pipe", None, "expert"),
            P("pipe", "expert", None),
            P("pipe", None, None),
            P("pipe", None),
        ),
        out_specs=P("pipe", None, "expert", None),
        check_vma=False,
    )
```

```python
import functools

import jax
import jax.numpy as jnp
from jax import lax
from jax.experimental import pallas as pl
from jax.experimental.pallas import tpu as pltpu
from jax.sharding import PartitionSpec as P

ROUTE_SCALE = 2.5
EPSILON = 1e-06
HIGHEST = lax.Precision.HIGHEST
F32 = jnp.float32
BF16 = jnp.bfloat16
D = 3584
EXPERTS = 8
CAP = 16
TOKENS = 64
SLOTS = EXPERTS * CAP
SLICE = 256
WIDE = D + 128
UNIT = 2 * CAP
NT = (((1,), (1,)), ((), ()))
TN = (((0,), (0,)), ((), ()))
COST = 100_000
WORK = 2_000_000_000
LIMIT = 16 * 1024 * 1024

VMEM = pl.BlockSpec(memory_space=pltpu.VMEM)
SMEM = pl.BlockSpec(memory_space=pltpu.SMEM)


def pipe_shift(value, by):
    return lax.ppermute(value, "pipe", [(i, (i + by) % 8) for i in range(8)])


def z_shift(value, by):
    pairs = [(i, ((i // 4 + by) % 8) * 4 + i % 4) for i in range(32)]
    return lax.ppermute(value, "expert", pairs)


def x_swap(value):
    return lax.ppermute(value, "expert", [(i, i ^ 2) for i in range(32)])


def core_swap(value):
    return lax.ppermute(value, "expert", [(i, i ^ 1) for i in range(32)])


def call(kernel, outs, specs, flops, moved):
    return pl.pallas_call(
        kernel,
        out_shape=outs,
        in_specs=specs,
        out_specs=jax.tree.map(lambda _: VMEM, outs),
        cost_estimate=pl.CostEstimate(flops=flops, bytes_accessed=moved, transcendentals=0),
        compiler_params=pltpu.CompilerParams(vmem_limit_bytes=LIMIT),
    )


def lanes(value_hi, value_lo, shape):
    lane = lax.broadcasted_iota(jnp.int32, shape, 1)
    return jnp.where(lane == 0, value_hi, jnp.where(lane == 1, value_lo, 0.0))


def split_sum(tile):
    total = jnp.sum(tile, axis=-1, keepdims=True)
    high = total.astype(BF16).astype(F32)
    return high, total - high


def prep_kernel(place, limits, routes, saved, gain, router, match, weight, scores, inv):
    z = place[0]
    slot = lax.broadcasted_iota(jnp.int32, (SLOTS, TOKENS), 0)
    expert = ((slot >> 4) + z) & (EXPERTS - 1)
    number = slot & (CAP - 1)
    limit = jnp.zeros((SLOTS, TOKENS), jnp.int32)
    for e in range(EXPERTS):
        limit = jnp.where(expert == e, limits[e], limit)
    allowed = number < limit
    earlier = (
        lax.broadcasted_iota(jnp.int32, (TOKENS, TOKENS), 0)
        < lax.broadcasted_iota(jnp.int32, (TOKENS, TOKENS), 1)
    ).astype(BF16)
    names = lax.broadcasted_iota(jnp.int32, (EXPERTS, TOKENS), 0)
    for m in range(2):
        values = saved[m].astype(F32)
        inv_rms = lax.rsqrt(jnp.mean(values * values, axis=-1, keepdims=True) + EPSILON)
        inv[m] = inv_rms
        normed = values * inv_rms * gain[...]
        logits = lax.dot_general(
            router[...], normed, NT, precision=HIGHEST, preferred_element_type=F32
        )
        score = jax.nn.sigmoid(logits)
        scores[m] = score
        picked = [routes[m, k : k + 1, :] == expert for k in range(2)]
        chosen = [
            jnp.sum(jnp.where(routes[m, k : k + 1, :] == names, score, 0.0), axis=0, keepdims=True)
            for k in range(2)
        ]
        totals = chosen[0] + chosen[1]
        counts = picked[0].astype(F32) + picked[1].astype(F32)
        before = jnp.dot(counts.astype(BF16), earlier, preferred_element_type=F32)
        kept = allowed & (before.astype(jnp.int32) == number)
        column = jnp.zeros((SLOTS, 1), F32)
        for k in range(2):
            hit = (picked[k] & kept).astype(F32)
            match[m, k] = hit
            share = (ROUTE_SCALE * chosen[k] / totals).astype(BF16).astype(F32)
            column = column + jnp.sum(hit * share, axis=-1, keepdims=True)
        weight[m] = column


def spread_kernel(first, second, match, weight, kept, *outs):
    for m, rows in enumerate((first, second)):
        kept[m] = rows[...]
        both = (match[m, 0] + match[m, 1]).astype(BF16)
        filled = jnp.dot(both, rows[...], preferred_element_type=F32)
        filled = (filled * weight[m]).astype(BF16)
        for k in range(EXPERTS):
            outs[k][m * CAP : (m + 1) * CAP] = filled[k * CAP : (k + 1) * CAP]


def stage_kernel(w_down, w_gate, w_up, packed):
    step = 512
    packed[:SLICE] = w_down[0]
    for at in range(0, D, step):
        packed[SLICE : 2 * SLICE, at : at + step] = w_gate[0, at : at + step].T
        packed[2 * SLICE :, at : at + step] = w_up[0, at : at + step].T


def pack_kernel(low, high, out):
    out[:UNIT] = low[...]
    out[UNIT:] = high[...]


def unit_kernel(shifts, place, mine, theirs, *refs):
    saved, weights = refs[0:2], refs[2:4]
    own, away, rows = refs[4:]
    n = len(shifts)
    z, x = place[0], place[1]
    size = UNIT * 2 * n
    half = size // 2
    rows[:half] = mine[...]
    rows[half:] = theirs[...]
    total = jnp.zeros((size, 1), F32)
    grads = []
    for s in range(2):
        parts = [[], []]
        for side in range(2):
            for shift in shifts:
                source = (z + 8 - shift) & 7
                column = x if side == 0 else 1 - x
                for part in range(2):
                    parts[part].append(saved[s][source, column, part].reshape(UNIT, SLICE))
        gate = jnp.concatenate(parts[0], axis=0).astype(F32)
        up = jnp.concatenate(parts[1], axis=0).astype(F32)
        projected = lax.dot_general(
            rows[...], weights[s][:SLICE], NT, preferred_element_type=F32
        )
        sig = jax.nn.sigmoid(gate)
        act = gate * sig
        total = total + jnp.sum(projected * (act * up), axis=-1, keepdims=True)
        gate_grad = (projected * up * sig * (1.0 + gate * (1.0 - sig))).astype(BF16)
        grads.append(jnp.concatenate([gate_grad, (projected * act).astype(BF16)], axis=1))
    step = 512
    for at in range(0, D, step):
        part = jnp.dot(grads[0], weights[0][SLICE:, at : at + step], preferred_element_type=F32)
        part = part + jnp.dot(
            grads[1], weights[1][SLICE:, at : at + step], preferred_element_type=F32
        )
        own[:, at : at + step] = part[:half]
        away[:, at : at + step] = part[half:].astype(BF16)
    high, low = split_sum(total)
    tile = lanes(high, low, (size, 128))
    own[:, D:] = tile[:half]
    away[:, D:] = tile[half:].astype(BF16)


def add_kernel(own, got, *outs):
    for i, out in enumerate(outs):
        at = slice(i * UNIT, (i + 1) * UNIT)
        out[:, :D] = (own[at, :D] + got[at, :D].astype(F32)).astype(BF16)
        high, low = split_sum(own[at, D:] + got[at, D:].astype(F32))
        out[:, D:] = lanes(high, low, (UNIT, 128)).astype(BF16)


def add_two_kernel(own, got, own_next, got_next, low, high, last):
    add_kernel(own, got, low, high)
    add_kernel(own_next, got_next, last)


def gather_kernel(own, got, b1, b7, b4, b3, b5, match, total, slot_dw, back):
    units = {1: b1, 7: b7, 4: b4, 3: b3, 5: b5}
    for m in range(2):
        at = slice(m * CAP, (m + 1) * CAP)
        back[:CAP] = (own[at, :D] + got[at, :D].astype(F32)).astype(BF16)
        dws = [own[at, D:] + got[at, D:].astype(F32)]
        for k in range(1, EXPERTS):
            rows = slice(k * CAP, (k + 1) * CAP)
            if k in units:
                back[rows] = units[k][at, :D]
                dws.append(units[k][at, D:].astype(F32))
            else:
                back[rows] = jnp.zeros((CAP, D), BF16)
                dws.append(jnp.zeros((CAP, 128), F32))
        slot_dw[m] = jnp.sum(jnp.concatenate(dws, axis=0), axis=-1, keepdims=True)
        both = (match[m, 0] + match[m, 1]).astype(BF16)
        total[m] = lax.dot_general(both, back[...], TN, preferred_element_type=F32)


def finish_kernel(
    b2, b6, some, some_dw, kept, saved, routes, match, weight, scores, inv, gain, router, out, back
):
    names = lax.broadcasted_iota(jnp.int32, (EXPERTS, TOKENS), 0)
    low, high = slice(2 * CAP, 3 * CAP), slice(6 * CAP, 7 * CAP)
    for m in range(2):
        finish_part(
            m, b2, b6, some, some_dw, kept, saved, routes, match, weight, scores, inv, gain,
            router, out, back, names, low, high,
        )


def finish_part(
    m, b2, b6, some, some_dw, kept, saved, routes, match, weight, scores, inv, gain, router, out,
    back, names, low, high,
):
    at = slice(m * CAP, (m + 1) * CAP)
    back[:CAP] = b2[at, :D]
    back[CAP:] = b6[at, :D]
    late = [jnp.sum(unit[at, D:].astype(F32), axis=-1, keepdims=True) for unit in (b2, b6)]
    slot_dw = some_dw[m]
    slot_dw = jnp.concatenate(
        [slot_dw[: low.start], late[0], slot_dw[low.stop : high.start], late[1], slot_dw[high.stop :]],
        axis=0,
    )
    share = weight[m]
    used = share > 0.0
    slot_dw = jnp.where(used, slot_dw / jnp.where(used, share, 1.0), 0.0)
    score = scores[m]
    chosen, choice, picked = [], [], []
    for k in range(2):
        picked.append(routes[m, k : k + 1, :] == names)
        chosen.append(jnp.sum(jnp.where(picked[k], score, 0.0), axis=0, keepdims=True))
        choice.append(jnp.sum(match[m, k] * slot_dw, axis=0, keepdims=True))
    totals = chosen[0] + chosen[1]
    inner = (choice[0] * chosen[0] + choice[1] * chosen[1]) / (totals * totals)
    score_grad = jnp.zeros((EXPERTS, TOKENS), F32)
    for k in range(2):
        slope = ROUTE_SCALE * (choice[k] / totals - inner)
        score_grad = score_grad + jnp.where(picked[k], slope, 0.0)
    score_grad = score_grad * score * (1.0 - score)
    both = (match[m, 0] + match[m, 1]).astype(BF16)
    both = jnp.concatenate([both[low], both[high]], axis=0)
    total = some[m] + lax.dot_general(both, back[...], TN, preferred_element_type=F32)
    total = total + lax.dot_general(
        score_grad, router[...], TN, precision=HIGHEST, preferred_element_type=F32
    )
    scaled = gain[...] * total
    values = saved[m].astype(F32)
    inv_rms = inv[m]
    mean = jnp.mean(values * scaled, axis=-1, keepdims=True)
    out[m] = (
        kept[m].astype(F32)
        + inv_rms * scaled
        - (inv_rms * inv_rms * inv_rms * mean) * values
    ).astype(BF16)


def shape(dims, dtype=BF16):
    return jax.ShapeDtypeStruct(dims, dtype)


def local(
    grads_sent, saved_in, routes, capacity, saved_pre, w_gate, w_up, w_down, router, norm_gain
):
    index = lax.axis_index("expert")
    core = index % 2
    place = jnp.stack([index // 4, (index // 2) % 2]).astype(jnp.int32)
    first, second = lax.optimization_barrier((grads_sent[0, 0], grads_sent[0, 1]))
    first, second = pipe_shift(first, -1), pipe_shift(second, 1)
    packed = call(stage_kernel, shape((3 * SLICE, D)), [VMEM] * 3, COST, 1000)(
        w_down, w_gate, w_up
    )
    pre = saved_pre[0].reshape(2, 8, 2, 2, CAP, 2, SLICE)
    pre = jnp.transpose(pre, (3, 1, 2, 5, 0, 4, 6))
    routes_t = jnp.transpose(routes[0], (0, 2, 1))
    router_t = router[0].T
    match, weight, scores, inv = call(
        prep_kernel,
        (
            shape((2, 2, SLOTS, TOKENS), F32),
            shape((2, SLOTS, 1), F32),
            shape((2, EXPERTS, TOKENS), F32),
            shape((2, TOKENS, 1), F32),
        ),
        [SMEM, SMEM] + [VMEM] * 4,
        COST,
        1000,
    )(place, capacity[0], routes_t, saved_in[0], norm_gain, router_t)
    pre_own = lax.dynamic_index_in_dim(pre, core, 0, keepdims=False)
    pre_other = lax.dynamic_index_in_dim(pre, 1 - core, 0, keepdims=False)
    first, second, packed, pre_own, pre_other, weight = lax.optimization_barrier(
        (first, second, packed, pre_own, pre_other, weight)
    )
    pre_other, weights = core_swap(pre_other), (packed, core_swap(packed))
    kept, *units = call(
        spread_kernel,
        (shape((2, TOKENS, D)),) + tuple(shape((UNIT, D)) for _ in range(EXPERTS)),
        [VMEM] * 4,
        COST,
        1000,
    )(first, second, match, weight)
    def work(group, mine, theirs):
        n = len(group)
        return pl.pallas_call(
            functools.partial(unit_kernel, group),
            out_shape=(shape((UNIT * n, WIDE), F32), shape((UNIT * n, WIDE))),
            in_specs=[SMEM] + [VMEM] * 6,
            out_specs=(VMEM, VMEM),
            scratch_shapes=[pltpu.VMEM((2 * UNIT * n, D), BF16)],
            cost_estimate=pl.CostEstimate(flops=WORK, bytes_accessed=1000, transcendentals=0),
            compiler_params=pltpu.CompilerParams(vmem_limit_bytes=LIMIT),
        )(place, mine, theirs, pre_own, pre_other, *weights)

    def add(group, own, got):
        return call(add_kernel, tuple(shape((UNIT, WIDE)) for _ in group), [VMEM] * 2, COST, 1000)(
            own, got
        )

    def pack(low, high):
        return call(pack_kernel, shape((2 * UNIT, D)), [VMEM] * 2, COST, 1000)(low, high)

    v = {"u%d" % k: units[k] for k in range(EXPERTS)}

    def tie(*names):
        v.update(zip(names, lax.optimization_barrier(tuple(v[n] for n in names))))

    def z_out(*shifts):
        for k in shifts:
            v["m%d" % k] = z_shift(v["u%d" % k], k)

    def z_back(*shifts):
        for k in shifts:
            v["b%d" % k] = z_shift(v["d%d" % k], -k)

    z_out(1, 7)
    v["t0"] = x_swap(v["u0"])
    tie("t0", "u0", "m1", "m7", "u4", "u3", "u5", "u2", "u6")
    z_out(4)
    v["p1"] = pack(v["m1"], v["m7"])
    v["t1"] = x_swap(v["p1"])
    v["own1"], v["away1"] = work((1, 7), v["p1"], v["t1"])
    tie("m4", "own1", "away1", "t0", "u0", "u3", "u5", "u2", "u6")
    z_out(3, 5)
    v["t4"] = x_swap(v["m4"])
    v["got1"] = x_swap(v["away1"])
    v["own4"], v["away4"] = work((4,), v["m4"], v["t4"])
    tie("got1", "own1", "own4", "away4", "m3", "m5", "t0", "u0", "u2", "u6")
    z_out(2, 6)
    v["p3"] = pack(v["m3"], v["m5"])
    v["t3"] = x_swap(v["p3"])
    v["got4"] = x_swap(v["away4"])
    v["own3"], v["away3"] = work((3, 5), v["p3"], v["t3"])
    tie("own3", "away3", "m2", "m6", "got4", "own4", "got1", "own1", "t0", "u0")
    v["d1"], v["d7"], v["d4"] = call(
        add_two_kernel, tuple(shape((UNIT, WIDE)) for _ in range(3)), [VMEM] * 4, COST, 1000
    )(v["own1"], v["got1"], v["own4"], v["got4"])
    z_back(1, 7, 4)
    v["p2"] = pack(v["m2"], v["m6"])
    v["t2"] = x_swap(v["p2"])
    v["got3"] = x_swap(v["away3"])
    v["own2"], v["away2"] = work((2, 6), v["p2"], v["t2"])
    v["own0"], v["away0"] = work((0,), v["u0"], v["t0"])
    tie("b1", "b7", "b4", "got3", "own3", "own2", "away2", "own0", "away0")
    v["d3"], v["d5"] = add((3, 5), v["own3"], v["got3"])
    z_back(3, 5)
    v["got2"] = x_swap(v["away2"])
    v["got0"] = x_swap(v["away0"])
    tie("b3", "b5", "got2", "own2", "got0", "own0")
    v["d2"], v["d6"] = add((2, 6), v["own2"], v["got2"])
    z_back(2, 6)
    some, some_dw = pl.pallas_call(
        gather_kernel,
        out_shape=(shape((2, TOKENS, D), F32), shape((2, SLOTS, 1), F32)),
        in_specs=[VMEM] * 8,
        out_specs=(VMEM, VMEM),
        scratch_shapes=[pltpu.VMEM((SLOTS, D), BF16)],
        cost_estimate=pl.CostEstimate(flops=COST, bytes_accessed=1000, transcendentals=0),
        compiler_params=pltpu.CompilerParams(vmem_limit_bytes=LIMIT),
    )(v["own0"], v["got0"], v["b1"], v["b7"], v["b4"], v["b3"], v["b5"], match)
    out = pl.pallas_call(
        finish_kernel,
        out_shape=shape((2, TOKENS, D)),
        in_specs=[VMEM] * 13,
        out_specs=VMEM,
        scratch_shapes=[pltpu.VMEM((2 * CAP, D), BF16)],
        cost_estimate=pl.CostEstimate(flops=COST, bytes_accessed=1000, transcendentals=0),
        compiler_params=pltpu.CompilerParams(vmem_limit_bytes=LIMIT),
    )(
        v["b2"],
        v["b6"],
        some,
        some_dw,
        kept,
        saved_in[0],
        routes_t,
        match,
        weight,
        scores,
        inv,
        norm_gain,
        router_t,
    )
    return out[None]


def solution(mesh):
    return jax.shard_map(
        local,
        mesh=mesh,
        in_specs=(
            P("pipe", None, "expert", None),
            P("pipe", None, "expert", None),
            P("pipe", None, "expert", None),
            P("pipe", None),
            P("pipe", None, None, None, None, "expert"),
            P("pipe", None, "expert"),
            P("pipe", None, "expert"),
            P("pipe", "expert", None),
            P("pipe", None, None),
            P("pipe", None),
        ),
        out_specs=P("pipe", None, "expert", None),
        check_vma=False,
    )
```

```python
import functools

import jax
import jax.numpy as jnp
from jax import lax
from jax.experimental import pallas as pl
from jax.experimental.pallas import tpu as pltpu
from jax.sharding import PartitionSpec as P

ROUTE_SCALE = 2.5
EPSILON = 1e-06
HIGHEST = lax.Precision.HIGHEST
F32 = jnp.float32
BF16 = jnp.bfloat16
D = 3584
EXPERTS = 8
CAP = 16
TOKENS = 64
SLOTS = EXPERTS * CAP
SLICE = 256
WIDE = D + 128
UNIT = 2 * CAP
NT = (((1,), (1,)), ((), ()))
TN = (((0,), (0,)), ((), ()))
COST = 100_000
WORK = 2_000_000_000
LIMIT = 16 * 1024 * 1024

VMEM = pl.BlockSpec(memory_space=pltpu.VMEM)
SMEM = pl.BlockSpec(memory_space=pltpu.SMEM)


def pipe_shift(value, by):
    return lax.ppermute(value, "pipe", [(i, (i + by) % 8) for i in range(8)])


def z_shift(value, by):
    pairs = [(i, ((i // 4 + by) % 8) * 4 + i % 4) for i in range(32)]
    return lax.ppermute(value, "expert", pairs)


def x_swap(value):
    return lax.ppermute(value, "expert", [(i, i ^ 2) for i in range(32)])


def core_swap(value):
    return lax.ppermute(value, "expert", [(i, i ^ 1) for i in range(32)])


def call(kernel, outs, specs, flops, moved):
    return pl.pallas_call(
        kernel,
        out_shape=outs,
        in_specs=specs,
        out_specs=jax.tree.map(lambda _: VMEM, outs),
        cost_estimate=pl.CostEstimate(flops=flops, bytes_accessed=moved, transcendentals=0),
        compiler_params=pltpu.CompilerParams(vmem_limit_bytes=LIMIT),
    )


def lanes(value_hi, value_lo, shape):
    lane = lax.broadcasted_iota(jnp.int32, shape, 1)
    return jnp.where(lane == 0, value_hi, jnp.where(lane == 1, value_lo, 0.0))


def split_sum(tile):
    total = jnp.sum(tile, axis=-1, keepdims=True)
    high = total.astype(BF16).astype(F32)
    return high, total - high


def prep_kernel(
    place, limits, routes, saved, gain, router, match, weight, scores, inv, parts
):
    z = place[0]
    high = router[...].astype(BF16).astype(F32)
    low = router[...] - high
    parts[...] = jnp.concatenate([high, high, low, jnp.zeros_like(low)], axis=0).astype(BF16)
    slot = lax.broadcasted_iota(jnp.int32, (SLOTS, TOKENS), 0)
    expert = ((slot >> 4) + z) & (EXPERTS - 1)
    number = slot & (CAP - 1)
    limit = jnp.zeros((SLOTS, TOKENS), jnp.int32)
    for e in range(EXPERTS):
        limit = jnp.where(expert == e, limits[e], limit)
    allowed = number < limit
    earlier = (
        lax.broadcasted_iota(jnp.int32, (TOKENS, TOKENS), 0)
        < lax.broadcasted_iota(jnp.int32, (TOKENS, TOKENS), 1)
    ).astype(BF16)
    names = lax.broadcasted_iota(jnp.int32, (EXPERTS, TOKENS), 0)
    for m in range(2):
        values = saved[m].astype(F32)
        inv_rms = lax.rsqrt(jnp.mean(values * values, axis=-1, keepdims=True) + EPSILON)
        inv[m] = inv_rms
        normed = values * inv_rms * gain[...]
        logits = lax.dot_general(
            router[...], normed, NT, precision=HIGHEST, preferred_element_type=F32
        )
        score = jax.nn.sigmoid(logits)
        scores[m] = score
        picked = [routes[m, k : k + 1, :] == expert for k in range(2)]
        chosen = [
            jnp.sum(jnp.where(routes[m, k : k + 1, :] == names, score, 0.0), axis=0, keepdims=True)
            for k in range(2)
        ]
        totals = chosen[0] + chosen[1]
        counts = picked[0].astype(F32) + picked[1].astype(F32)
        before = jnp.dot(counts.astype(BF16), earlier, preferred_element_type=F32)
        kept = allowed & (before.astype(jnp.int32) == number)
        column = jnp.zeros((SLOTS, 1), F32)
        for k in range(2):
            hit = (picked[k] & kept).astype(F32)
            match[m, k] = hit
            share = (ROUTE_SCALE * chosen[k] / totals).astype(BF16).astype(F32)
            column = column + jnp.sum(hit * share, axis=-1, keepdims=True)
        weight[m] = column


def split_kernel(sent, first, second, sems):
    copies = [
        pltpu.make_async_copy(sent.at[0, m], out, sems.at[m])
        for m, out in enumerate((first, second))
    ]
    for copy in copies:
        copy.start()
    for copy in copies:
        copy.wait()


def spread_kernel(first, second, match, weight, kept, *outs):
    for m, rows in enumerate((first, second)):
        kept[m] = rows[...]
        both = (match[m, 0] + match[m, 1]).astype(BF16)
        filled = jnp.dot(both, rows[...], preferred_element_type=F32)
        filled = (filled * weight[m]).astype(BF16)
        for k in range(EXPERTS):
            outs[k][m * CAP : (m + 1) * CAP] = filled[k * CAP : (k + 1) * CAP]


def stage_kernel(w_down, w_gate, w_up, packed):
    step = 512
    packed[:SLICE] = w_down[0]
    for at in range(0, D, step):
        packed[SLICE : 2 * SLICE, at : at + step] = w_gate[0, at : at + step].T
        packed[2 * SLICE :, at : at + step] = w_up[0, at : at + step].T


def pack_kernel(low, high, out):
    out[:UNIT] = low[...]
    out[UNIT:] = high[...]


def unit_kernel(shifts, place, mine, theirs, *refs):
    saved, weights = refs[0:2], refs[2:4]
    own, away, rows = refs[4:]
    n = len(shifts)
    z, x = place[0], place[1]
    size = UNIT * 2 * n
    half = size // 2
    rows[:half] = mine[...]
    rows[half:] = theirs[...]
    total = jnp.zeros((size, 1), F32)
    grads = []
    for s in range(2):
        parts = [[], []]
        for side in range(2):
            for shift in shifts:
                source = (z + 8 - shift) & 7
                column = x if side == 0 else 1 - x
                for part in range(2):
                    parts[part].append(saved[s][source, column, part].reshape(UNIT, SLICE))
        gate = jnp.concatenate(parts[0], axis=0).astype(F32)
        up = jnp.concatenate(parts[1], axis=0).astype(F32)
        projected = lax.dot_general(
            rows[...], weights[s][:SLICE], NT, preferred_element_type=F32
        )
        sig = jax.nn.sigmoid(gate)
        act = gate * sig
        total = total + jnp.sum(projected * (act * up), axis=-1, keepdims=True)
        gate_grad = (projected * up * sig * (1.0 + gate * (1.0 - sig))).astype(BF16)
        grads.append(jnp.concatenate([gate_grad, (projected * act).astype(BF16)], axis=1))
    step = 512
    for at in range(0, D, step):
        part = jnp.dot(grads[0], weights[0][SLICE:, at : at + step], preferred_element_type=F32)
        part = part + jnp.dot(
            grads[1], weights[1][SLICE:, at : at + step], preferred_element_type=F32
        )
        own[:, at : at + step] = part[:half]
        away[:, at : at + step] = part[half:].astype(BF16)
    high, low = split_sum(total)
    tile = lanes(high, low, (size, 128))
    own[:, D:] = tile[:half]
    away[:, D:] = tile[half:].astype(BF16)


def add_kernel(own, got, *outs):
    for i, out in enumerate(outs):
        at = slice(i * UNIT, (i + 1) * UNIT)
        out[:, :D] = (own[at, :D] + got[at, :D].astype(F32)).astype(BF16)
        high, low = split_sum(own[at, D:] + got[at, D:].astype(F32))
        out[:, D:] = lanes(high, low, (UNIT, 128)).astype(BF16)


def add_two_kernel(own, got, own_next, got_next, low, high, last):
    add_kernel(own, got, low, high)
    add_kernel(own_next, got_next, last)


def gather_kernel(own, got, b1, b7, b4, b3, b5, match, total, slot_dw, back):
    units = {1: b1, 7: b7, 4: b4, 3: b3, 5: b5}
    for m in range(2):
        at = slice(m * CAP, (m + 1) * CAP)
        back[:CAP] = (own[at, :D] + got[at, :D].astype(F32)).astype(BF16)
        dws = [own[at, D:] + got[at, D:].astype(F32)]
        for k in range(1, EXPERTS):
            rows = slice(k * CAP, (k + 1) * CAP)
            if k in units:
                back[rows] = units[k][at, :D]
                dws.append(units[k][at, D:].astype(F32))
            else:
                back[rows] = jnp.zeros((CAP, D), BF16)
                dws.append(jnp.zeros((CAP, 128), F32))
        slot_dw[m] = jnp.sum(jnp.concatenate(dws, axis=0), axis=-1, keepdims=True)
        both = (match[m, 0] + match[m, 1]).astype(BF16)
        total[m] = lax.dot_general(both, back[...], TN, preferred_element_type=F32)


def finish_kernel(
    b2, b6, some, some_dw, kept, saved, routes, match, weight, scores, inv, gain, parts, out, back
):
    names = lax.broadcasted_iota(jnp.int32, (EXPERTS, TOKENS), 0)
    low, high = slice(2 * CAP, 3 * CAP), slice(6 * CAP, 7 * CAP)
    back[2 * CAP :] = parts[...]
    for m in range(2):
        finish_part(
            m, b2, b6, some, some_dw, kept, saved, routes, match, weight, scores, inv, gain,
            out, back, names, low, high,
        )


def finish_part(
    m, b2, b6, some, some_dw, kept, saved, routes, match, weight, scores, inv, gain, out,
    back, names, low, high,
):
    at = slice(m * CAP, (m + 1) * CAP)
    back[:CAP] = b2[at, :D]
    back[CAP : 2 * CAP] = b6[at, :D]
    late = [jnp.sum(unit[at, D:].astype(F32), axis=-1, keepdims=True) for unit in (b2, b6)]
    slot_dw = some_dw[m]
    slot_dw = jnp.concatenate(
        [slot_dw[: low.start], late[0], slot_dw[low.stop : high.start], late[1], slot_dw[high.stop :]],
        axis=0,
    )
    share = weight[m]
    used = share > 0.0
    slot_dw = jnp.where(used, slot_dw / jnp.where(used, share, 1.0), 0.0)
    score = scores[m]
    chosen, choice, picked = [], [], []
    for k in range(2):
        picked.append(routes[m, k : k + 1, :] == names)
        chosen.append(jnp.sum(jnp.where(picked[k], score, 0.0), axis=0, keepdims=True))
        choice.append(jnp.sum(match[m, k] * slot_dw, axis=0, keepdims=True))
    totals = chosen[0] + chosen[1]
    inner = (choice[0] * chosen[0] + choice[1] * chosen[1]) / (totals * totals)
    score_grad = jnp.zeros((EXPERTS, TOKENS), F32)
    for k in range(2):
        slope = ROUTE_SCALE * (choice[k] / totals - inner)
        score_grad = score_grad + jnp.where(picked[k], slope, 0.0)
    score_grad = score_grad * score * (1.0 - score)
    both = match[m, 0] + match[m, 1]
    main = score_grad.astype(BF16).astype(F32)
    rest = score_grad - main
    both = jnp.concatenate(
        [both[low], both[high], main, rest, main, jnp.zeros_like(main)], axis=0
    ).astype(BF16)
    total = some[m] + lax.dot_general(both, back[...], TN, preferred_element_type=F32)
    scaled = gain[...] * total
    values = saved[m].astype(F32)
    inv_rms = inv[m]
    mean = jnp.mean(values * scaled, axis=-1, keepdims=True)
    out[m] = (
        kept[m].astype(F32)
        + inv_rms * scaled
        - (inv_rms * inv_rms * inv_rms * mean) * values
    ).astype(BF16)


def shape(dims, dtype=BF16):
    return jax.ShapeDtypeStruct(dims, dtype)


def local(
    grads_sent, saved_in, routes, capacity, saved_pre, w_gate, w_up, w_down, router, norm_gain
):
    index = lax.axis_index("expert")
    core = index % 2
    place = jnp.stack([index // 4, (index // 2) % 2]).astype(jnp.int32)
    first, second = pl.pallas_call(
        split_kernel,
        out_shape=(shape((TOKENS, D)), shape((TOKENS, D))),
        in_specs=[pl.BlockSpec(memory_space=pl.ANY)],
        out_specs=(VMEM, VMEM),
        scratch_shapes=[pltpu.SemaphoreType.DMA((2,))],
        cost_estimate=pl.CostEstimate(flops=COST, bytes_accessed=1000, transcendentals=0),
        compiler_params=pltpu.CompilerParams(vmem_limit_bytes=LIMIT),
    )(grads_sent)
    first, second = pipe_shift(first, -1), pipe_shift(second, 1)
    packed = call(stage_kernel, shape((3 * SLICE, D)), [VMEM] * 3, COST, 1000)(
        w_down, w_gate, w_up
    )
    pre = saved_pre[0].reshape(2, 8, 2, 2, CAP, 2, SLICE)
    pre = jnp.transpose(pre, (3, 1, 2, 5, 0, 4, 6))
    routes_t = jnp.transpose(routes[0], (0, 2, 1))
    router_t = router[0].T
    match, weight, scores, inv, parts = call(
        prep_kernel,
        (
            shape((2, 2, SLOTS, TOKENS), F32),
            shape((2, SLOTS, 1), F32),
            shape((2, EXPERTS, TOKENS), F32),
            shape((2, TOKENS, 1), F32),
            shape((4 * EXPERTS, D)),
        ),
        [SMEM, SMEM] + [VMEM] * 4,
        COST,
        1000,
    )(place, capacity[0], routes_t, saved_in[0], norm_gain, router_t)
    pre_own = lax.dynamic_index_in_dim(pre, core, 0, keepdims=False)
    pre_other = lax.dynamic_index_in_dim(pre, 1 - core, 0, keepdims=False)
    first, second, packed, pre_own, pre_other, weight = lax.optimization_barrier(
        (first, second, packed, pre_own, pre_other, weight)
    )
    pre_other, weights = core_swap(pre_other), (packed, core_swap(packed))
    kept, *units = call(
        spread_kernel,
        (shape((2, TOKENS, D)),) + tuple(shape((UNIT, D)) for _ in range(EXPERTS)),
        [VMEM] * 4,
        COST,
        1000,
    )(first, second, match, weight)
    def work(group, mine, theirs):
        n = len(group)
        return pl.pallas_call(
            functools.partial(unit_kernel, group),
            out_shape=(shape((UNIT * n, WIDE), F32), shape((UNIT * n, WIDE))),
            in_specs=[SMEM] + [VMEM] * 6,
            out_specs=(VMEM, VMEM),
            scratch_shapes=[pltpu.VMEM((2 * UNIT * n, D), BF16)],
            cost_estimate=pl.CostEstimate(flops=WORK, bytes_accessed=1000, transcendentals=0),
            compiler_params=pltpu.CompilerParams(vmem_limit_bytes=LIMIT),
        )(place, mine, theirs, pre_own, pre_other, *weights)

    def add(group, own, got):
        return call(add_kernel, tuple(shape((UNIT, WIDE)) for _ in group), [VMEM] * 2, COST, 1000)(
            own, got
        )

    def pack(low, high):
        return call(pack_kernel, shape((2 * UNIT, D)), [VMEM] * 2, COST, 1000)(low, high)

    v = {"u%d" % k: units[k] for k in range(EXPERTS)}

    def tie(*names):
        v.update(zip(names, lax.optimization_barrier(tuple(v[n] for n in names))))

    def z_out(*shifts):
        for k in shifts:
            v["m%d" % k] = z_shift(v["u%d" % k], k)

    def z_back(*shifts):
        for k in shifts:
            v["b%d" % k] = z_shift(v["d%d" % k], -k)

    z_out(1, 7)
    v["t0"] = x_swap(v["u0"])
    tie("t0", "u0", "m1", "m7", "u4", "u3", "u5", "u2", "u6")
    z_out(4)
    v["p1"] = pack(v["m1"], v["m7"])
    v["t1"] = x_swap(v["p1"])
    v["own1"], v["away1"] = work((1, 7), v["p1"], v["t1"])
    tie("m4", "own1", "away1", "t0", "u0", "u3", "u5", "u2", "u6")
    z_out(3, 5)
    v["t4"] = x_swap(v["m4"])
    v["got1"] = x_swap(v["away1"])
    v["own4"], v["away4"] = work((4,), v["m4"], v["t4"])
    tie("got1", "own1", "own4", "away4", "m3", "m5", "t0", "u0", "u2", "u6")
    z_out(2, 6)
    v["p3"] = pack(v["m3"], v["m5"])
    v["t3"] = x_swap(v["p3"])
    v["got4"] = x_swap(v["away4"])
    v["own3"], v["away3"] = work((3, 5), v["p3"], v["t3"])
    tie("own3", "away3", "m2", "m6", "got4", "own4", "got1", "own1", "t0", "u0")
    v["d1"], v["d7"], v["d4"] = call(
        add_two_kernel, tuple(shape((UNIT, WIDE)) for _ in range(3)), [VMEM] * 4, COST, 1000
    )(v["own1"], v["got1"], v["own4"], v["got4"])
    z_back(1, 7, 4)
    v["p2"] = pack(v["m2"], v["m6"])
    v["t2"] = x_swap(v["p2"])
    v["got3"] = x_swap(v["away3"])
    v["own2"], v["away2"] = work((2, 6), v["p2"], v["t2"])
    v["own0"], v["away0"] = work((0,), v["u0"], v["t0"])
    tie("b1", "b7", "b4", "got3", "own3", "own2", "away2", "own0", "away0")
    v["d3"], v["d5"] = add((3, 5), v["own3"], v["got3"])
    z_back(3, 5)
    v["got2"] = x_swap(v["away2"])
    v["got0"] = x_swap(v["away0"])
    tie("got2", "own2")
    v["d2"], v["d6"] = add((2, 6), v["own2"], v["got2"])
    z_back(2, 6)
    some, some_dw = pl.pallas_call(
        gather_kernel,
        out_shape=(shape((2, TOKENS, D), F32), shape((2, SLOTS, 1), F32)),
        in_specs=[VMEM] * 8,
        out_specs=(VMEM, VMEM),
        scratch_shapes=[pltpu.VMEM((SLOTS, D), BF16)],
        cost_estimate=pl.CostEstimate(flops=COST, bytes_accessed=1000, transcendentals=0),
        compiler_params=pltpu.CompilerParams(vmem_limit_bytes=LIMIT),
    )(v["own0"], v["got0"], v["b1"], v["b7"], v["b4"], v["b3"], v["b5"], match)
    out = pl.pallas_call(
        finish_kernel,
        out_shape=shape((2, TOKENS, D)),
        in_specs=[VMEM] * 13,
        out_specs=VMEM,
        scratch_shapes=[pltpu.VMEM((2 * CAP + 4 * EXPERTS, D), BF16)],
        cost_estimate=pl.CostEstimate(flops=COST, bytes_accessed=1000, transcendentals=0),
        compiler_params=pltpu.CompilerParams(vmem_limit_bytes=LIMIT),
    )(
        v["b2"],
        v["b6"],
        some,
        some_dw,
        kept,
        saved_in[0],
        routes_t,
        match,
        weight,
        scores,
        inv,
        norm_gain,
        parts,
    )
    return out[None]


def solution(mesh):
    return jax.shard_map(
        local,
        mesh=mesh,
        in_specs=(
            P("pipe", None, "expert", None),
            P("pipe", None, "expert", None),
            P("pipe", None, "expert", None),
            P("pipe", None),
            P("pipe", None, None, None, None, "expert"),
            P("pipe", None, "expert"),
            P("pipe", None, "expert"),
            P("pipe", "expert", None),
            P("pipe", None, None),
            P("pipe", None),
        ),
        out_specs=P("pipe", None, "expert", None),
        check_vma=False,
    )
```

```python
import functools

import jax
import jax.numpy as jnp
from jax import lax
from jax.experimental import pallas as pl
from jax.experimental.pallas import tpu as pltpu
from jax.sharding import PartitionSpec as P

ROUTE_SCALE = 2.5
EPSILON = 1e-06
HIGHEST = lax.Precision.HIGHEST
F32 = jnp.float32
BF16 = jnp.bfloat16
D = 3584
EXPERTS = 8
CAP = 16
TOKENS = 64
SLOTS = EXPERTS * CAP
SLICE = 256
WIDE = D + 128
UNIT = 2 * CAP
NT = (((1,), (1,)), ((), ()))
TN = (((0,), (0,)), ((), ()))
COST = 100_000
SLOW = 20_000_000_000
WORK = 2_000_000_000
LIMIT = 16 * 1024 * 1024

VMEM = pl.BlockSpec(memory_space=pltpu.VMEM)
SMEM = pl.BlockSpec(memory_space=pltpu.SMEM)


def pipe_shift(value, by):
    return lax.ppermute(value, "pipe", [(i, (i + by) % 8) for i in range(8)])


def z_shift(value, by):
    pairs = [(i, ((i // 4 + by) % 8) * 4 + i % 4) for i in range(32)]
    return lax.ppermute(value, "expert", pairs)


def x_swap(value):
    return lax.ppermute(value, "expert", [(i, i ^ 2) for i in range(32)])


def core_swap(value):
    return lax.ppermute(value, "expert", [(i, i ^ 1) for i in range(32)])


def call(kernel, outs, specs, flops, moved):
    return pl.pallas_call(
        kernel,
        out_shape=outs,
        in_specs=specs,
        out_specs=jax.tree.map(lambda _: VMEM, outs),
        cost_estimate=pl.CostEstimate(flops=flops, bytes_accessed=moved, transcendentals=0),
        compiler_params=pltpu.CompilerParams(vmem_limit_bytes=LIMIT),
    )


def lanes(value_hi, value_lo, shape):
    lane = lax.broadcasted_iota(jnp.int32, shape, 1)
    return jnp.where(lane == 0, value_hi, jnp.where(lane == 1, value_lo, 0.0))


def split_sum(tile):
    total = jnp.sum(tile, axis=-1, keepdims=True)
    high = total.astype(BF16).astype(F32)
    return high, total - high


def prep_kernel(
    place, limits, routes, saved, gain, router, match, weight, scores, inv, parts
):
    z = place[0]
    high = router[...].astype(BF16).astype(F32)
    low = router[...] - high
    parts[...] = jnp.concatenate([high, high, low, jnp.zeros_like(low)], axis=0).astype(BF16)
    slot = lax.broadcasted_iota(jnp.int32, (SLOTS, TOKENS), 0)
    expert = ((slot >> 4) + z) & (EXPERTS - 1)
    number = slot & (CAP - 1)
    limit = jnp.zeros((SLOTS, TOKENS), jnp.int32)
    for e in range(EXPERTS):
        limit = jnp.where(expert == e, limits[e], limit)
    allowed = number < limit
    earlier = (
        lax.broadcasted_iota(jnp.int32, (TOKENS, TOKENS), 0)
        < lax.broadcasted_iota(jnp.int32, (TOKENS, TOKENS), 1)
    ).astype(BF16)
    names = lax.broadcasted_iota(jnp.int32, (EXPERTS, TOKENS), 0)
    for m in range(2):
        values = saved[m].astype(F32)
        inv_rms = lax.rsqrt(jnp.mean(values * values, axis=-1, keepdims=True) + EPSILON)
        inv[m] = inv_rms
        normed = values * inv_rms * gain[...]
        logits = lax.dot_general(
            router[...], normed, NT, precision=HIGHEST, preferred_element_type=F32
        )
        score = jax.nn.sigmoid(logits)
        scores[m] = score
        picked = [routes[m, k : k + 1, :] == expert for k in range(2)]
        chosen = [
            jnp.sum(jnp.where(routes[m, k : k + 1, :] == names, score, 0.0), axis=0, keepdims=True)
            for k in range(2)
        ]
        totals = chosen[0] + chosen[1]
        counts = picked[0].astype(F32) + picked[1].astype(F32)
        before = jnp.dot(counts.astype(BF16), earlier, preferred_element_type=F32)
        kept = allowed & (before.astype(jnp.int32) == number)
        column = jnp.zeros((SLOTS, 1), F32)
        for k in range(2):
            hit = (picked[k] & kept).astype(F32)
            match[m, k] = hit
            share = (ROUTE_SCALE * chosen[k] / totals).astype(BF16).astype(F32)
            column = column + jnp.sum(hit * share, axis=-1, keepdims=True)
        weight[m] = column


def split_kernel(sent, first, second, sems):
    copies = [
        pltpu.make_async_copy(sent.at[0, m], out, sems.at[m])
        for m, out in enumerate((first, second))
    ]
    for copy in copies:
        copy.start()
    for copy in copies:
        copy.wait()


def spread_kernel(first, second, match, weight, kept, *outs):
    for m, rows in enumerate((first, second)):
        kept[m] = rows[...]
        both = (match[m, 0] + match[m, 1]).astype(BF16)
        filled = jnp.dot(both, rows[...], preferred_element_type=F32)
        filled = (filled * weight[m]).astype(BF16)
        for k in range(EXPERTS):
            outs[k][m * CAP : (m + 1) * CAP] = filled[k * CAP : (k + 1) * CAP]


def stage_kernel(w_down, w_gate, w_up, packed):
    step = 512
    packed[:SLICE] = w_down[0]
    for at in range(0, D, step):
        packed[SLICE : 2 * SLICE, at : at + step] = w_gate[0, at : at + step].T
        packed[2 * SLICE :, at : at + step] = w_up[0, at : at + step].T


def pack_kernel(low, high, out):
    out[:UNIT] = low[...]
    out[UNIT:] = high[...]


def unit_kernel(shifts, place, mine, theirs, *refs):
    saved, weights = refs[0:2], refs[2:4]
    own, away, rows = refs[4:]
    n = len(shifts)
    z, x = place[0], place[1]
    size = UNIT * 2 * n
    half = size // 2
    rows[:half] = mine[...]
    rows[half:] = theirs[...]
    total = jnp.zeros((size, 1), F32)
    grads = []
    for s in range(2):
        parts = [[], []]
        for side in range(2):
            for shift in shifts:
                source = (z + 8 - shift) & 7
                column = x if side == 0 else 1 - x
                for part in range(2):
                    parts[part].append(saved[s][source, column, part].reshape(UNIT, SLICE))
        gate = jnp.concatenate(parts[0], axis=0).astype(F32)
        up = jnp.concatenate(parts[1], axis=0).astype(F32)
        projected = lax.dot_general(
            rows[...], weights[s][:SLICE], NT, preferred_element_type=F32
        )
        sig = jax.nn.sigmoid(gate)
        act = gate * sig
        total = total + jnp.sum(projected * (act * up), axis=-1, keepdims=True)
        gate_grad = (projected * up * sig * (1.0 + gate * (1.0 - sig))).astype(BF16)
        grads.append(jnp.concatenate([gate_grad, (projected * act).astype(BF16)], axis=1))
    step = 512
    for at in range(0, D, step):
        part = jnp.dot(grads[0], weights[0][SLICE:, at : at + step], preferred_element_type=F32)
        part = part + jnp.dot(
            grads[1], weights[1][SLICE:, at : at + step], preferred_element_type=F32
        )
        own[:, at : at + step] = part[:half]
        away[:, at : at + step] = part[half:].astype(BF16)
    high, low = split_sum(total)
    tile = lanes(high, low, (size, 128))
    own[:, D:] = tile[:half]
    away[:, D:] = tile[half:].astype(BF16)


def add_kernel(own, got, *outs):
    for i, out in enumerate(outs):
        at = slice(i * UNIT, (i + 1) * UNIT)
        out[:, :D] = (own[at, :D] + got[at, :D].astype(F32)).astype(BF16)
        high, low = split_sum(own[at, D:] + got[at, D:].astype(F32))
        out[:, D:] = lanes(high, low, (UNIT, 128)).astype(BF16)


def add_two_kernel(own, got, own_next, got_next, low, high, last):
    add_kernel(own, got, low, high)
    add_kernel(own_next, got_next, last)


def gather_kernel(own, got, b1, b7, b4, b3, b5, match, total, slot_dw, back):
    units = {1: b1, 7: b7, 4: b4, 3: b3, 5: b5}
    for m in range(2):
        at = slice(m * CAP, (m + 1) * CAP)
        back[:CAP] = (own[at, :D] + got[at, :D].astype(F32)).astype(BF16)
        dws = [own[at, D:] + got[at, D:].astype(F32)]
        for k in range(1, EXPERTS):
            rows = slice(k * CAP, (k + 1) * CAP)
            if k in units:
                back[rows] = units[k][at, :D]
                dws.append(units[k][at, D:].astype(F32))
            else:
                back[rows] = jnp.zeros((CAP, D), BF16)
                dws.append(jnp.zeros((CAP, 128), F32))
        slot_dw[m] = jnp.sum(jnp.concatenate(dws, axis=0), axis=-1, keepdims=True)
        both = (match[m, 0] + match[m, 1]).astype(BF16)
        total[m] = lax.dot_general(both, back[...], TN, preferred_element_type=F32)


def finish_kernel(
    b2, b6, some, some_dw, kept, saved, routes, match, weight, scores, inv, gain, parts, out, back
):
    names = lax.broadcasted_iota(jnp.int32, (EXPERTS, TOKENS), 0)
    low, high = slice(2 * CAP, 3 * CAP), slice(6 * CAP, 7 * CAP)
    back[2 * CAP :] = parts[...]
    for m in range(2):
        finish_part(
            m, b2, b6, some, some_dw, kept, saved, routes, match, weight, scores, inv, gain,
            out, back, names, low, high,
        )


def finish_part(
    m, b2, b6, some, some_dw, kept, saved, routes, match, weight, scores, inv, gain, out,
    back, names, low, high,
):
    at = slice(m * CAP, (m + 1) * CAP)
    back[:CAP] = b2[at, :D]
    back[CAP : 2 * CAP] = b6[at, :D]
    late = [jnp.sum(unit[at, D:].astype(F32), axis=-1, keepdims=True) for unit in (b2, b6)]
    slot_dw = some_dw[m]
    slot_dw = jnp.concatenate(
        [slot_dw[: low.start], late[0], slot_dw[low.stop : high.start], late[1], slot_dw[high.stop :]],
        axis=0,
    )
    share = weight[m]
    used = share > 0.0
    slot_dw = jnp.where(used, slot_dw / jnp.where(used, share, 1.0), 0.0)
    score = scores[m]
    chosen, choice, picked = [], [], []
    for k in range(2):
        picked.append(routes[m, k : k + 1, :] == names)
        chosen.append(jnp.sum(jnp.where(picked[k], score, 0.0), axis=0, keepdims=True))
        choice.append(jnp.sum(match[m, k] * slot_dw, axis=0, keepdims=True))
    totals = chosen[0] + chosen[1]
    inner = (choice[0] * chosen[0] + choice[1] * chosen[1]) / (totals * totals)
    score_grad = jnp.zeros((EXPERTS, TOKENS), F32)
    for k in range(2):
        slope = ROUTE_SCALE * (choice[k] / totals - inner)
        score_grad = score_grad + jnp.where(picked[k], slope, 0.0)
    score_grad = score_grad * score * (1.0 - score)
    both = match[m, 0] + match[m, 1]
    main = score_grad.astype(BF16).astype(F32)
    rest = score_grad - main
    both = jnp.concatenate(
        [both[low], both[high], main, rest, main, jnp.zeros_like(main)], axis=0
    ).astype(BF16)
    total = some[m] + lax.dot_general(both, back[...], TN, preferred_element_type=F32)
    scaled = gain[...] * total
    values = saved[m].astype(F32)
    inv_rms = inv[m]
    mean = jnp.mean(values * scaled, axis=-1, keepdims=True)
    out[m] = (
        kept[m].astype(F32)
        + inv_rms * scaled
        - (inv_rms * inv_rms * inv_rms * mean) * values
    ).astype(BF16)


def shape(dims, dtype=BF16):
    return jax.ShapeDtypeStruct(dims, dtype)


def local(
    grads_sent, saved_in, routes, capacity, saved_pre, w_gate, w_up, w_down, router, norm_gain
):
    index = lax.axis_index("expert")
    core = index % 2
    place = jnp.stack([index // 4, (index // 2) % 2]).astype(jnp.int32)
    first, second = pl.pallas_call(
        split_kernel,
        out_shape=(shape((TOKENS, D)), shape((TOKENS, D))),
        in_specs=[pl.BlockSpec(memory_space=pl.ANY)],
        out_specs=(VMEM, VMEM),
        scratch_shapes=[pltpu.SemaphoreType.DMA((2,))],
        cost_estimate=pl.CostEstimate(flops=COST, bytes_accessed=1000, transcendentals=0),
        compiler_params=pltpu.CompilerParams(vmem_limit_bytes=LIMIT),
    )(grads_sent)
    first, second = pipe_shift(first, -1), pipe_shift(second, 1)
    packed = call(stage_kernel, shape((3 * SLICE, D)), [VMEM] * 3, COST, 1000)(
        w_down, w_gate, w_up
    )
    pre = saved_pre[0].reshape(2, 8, 2, 2, CAP, 2, SLICE)
    pre = jnp.transpose(pre, (3, 1, 2, 5, 0, 4, 6))
    routes_t = jnp.transpose(routes[0], (0, 2, 1))
    router_t = router[0].T
    match, weight, scores, inv, parts = call(
        prep_kernel,
        (
            shape((2, 2, SLOTS, TOKENS), F32),
            shape((2, SLOTS, 1), F32),
            shape((2, EXPERTS, TOKENS), F32),
            shape((2, TOKENS, 1), F32),
            shape((4 * EXPERTS, D)),
        ),
        [SMEM, SMEM] + [VMEM] * 4,
        COST,
        1000,
    )(place, capacity[0], routes_t, saved_in[0], norm_gain, router_t)
    pre_own = lax.dynamic_index_in_dim(pre, core, 0, keepdims=False)
    pre_other = lax.dynamic_index_in_dim(pre, 1 - core, 0, keepdims=False)
    first, second, packed, pre_own, pre_other, weight = lax.optimization_barrier(
        (first, second, packed, pre_own, pre_other, weight)
    )
    pre_other, weights = core_swap(pre_other), (packed, core_swap(packed))
    kept, *units = call(
        spread_kernel,
        (shape((2, TOKENS, D)),) + tuple(shape((UNIT, D)) for _ in range(EXPERTS)),
        [VMEM] * 4,
        COST,
        1000,
    )(first, second, match, weight)
    def work(group, mine, theirs):
        n = len(group)
        return pl.pallas_call(
            functools.partial(unit_kernel, group),
            out_shape=(shape((UNIT * n, WIDE), F32), shape((UNIT * n, WIDE))),
            in_specs=[SMEM] + [VMEM] * 6,
            out_specs=(VMEM, VMEM),
            scratch_shapes=[pltpu.VMEM((2 * UNIT * n, D), BF16)],
            cost_estimate=pl.CostEstimate(flops=WORK, bytes_accessed=1000, transcendentals=0),
            compiler_params=pltpu.CompilerParams(vmem_limit_bytes=LIMIT),
        )(place, mine, theirs, pre_own, pre_other, *weights)

    def add(group, own, got, cost=COST):
        return call(add_kernel, tuple(shape((UNIT, WIDE)) for _ in group), [VMEM] * 2, cost, 1000)(
            own, got
        )

    def pack(low, high):
        return call(pack_kernel, shape((2 * UNIT, D)), [VMEM] * 2, COST, 1000)(low, high)

    v = {"u%d" % k: units[k] for k in range(EXPERTS)}

    def tie(*names):
        v.update(zip(names, lax.optimization_barrier(tuple(v[n] for n in names))))

    def z_out(*shifts):
        for k in shifts:
            v["m%d" % k] = z_shift(v["u%d" % k], k)

    def z_back(*shifts):
        for k in shifts:
            v["b%d" % k] = z_shift(v["d%d" % k], -k)

    z_out(1, 7)
    v["t0"] = x_swap(v["u0"])
    tie("m1", "m7", "u4", "u3", "u5", "u2", "u6", "t0", "u0")
    z_out(4)
    v["p1"] = pack(v["m1"], v["m7"])
    v["t1"] = x_swap(v["p1"])
    v["own1"], v["away1"] = work((1, 7), v["p1"], v["t1"])
    tie("m4", "own1", "away1", "t0", "u0", "u3", "u5", "u2", "u6")
    z_out(3, 5)
    v["t4"] = x_swap(v["m4"])
    v["got1"] = x_swap(v["away1"])
    v["own4"], v["away4"] = work((4,), v["m4"], v["t4"])
    tie("got1", "own1", "own4", "away4", "m3", "m5", "t0", "u0", "u2", "u6")
    z_out(2, 6)
    v["p3"] = pack(v["m3"], v["m5"])
    v["t3"] = x_swap(v["p3"])
    v["got4"] = x_swap(v["away4"])
    v["own3"], v["away3"] = work((3, 5), v["p3"], v["t3"])
    tie("own3", "away3", "m2", "m6", "got4", "own4", "got1", "own1", "t0", "u0")
    v["d1"], v["d7"], v["d4"] = call(
        add_two_kernel, tuple(shape((UNIT, WIDE)) for _ in range(3)), [VMEM] * 4, COST, 1000
    )(v["own1"], v["got1"], v["own4"], v["got4"])
    z_back(1, 7, 4)
    v["p2"] = pack(v["m2"], v["m6"])
    v["t2"] = x_swap(v["p2"])
    v["got3"] = x_swap(v["away3"])
    v["own2"], v["away2"] = work((2, 6), v["p2"], v["t2"])
    v["own0"], v["away0"] = work((0,), v["u0"], v["t0"])
    v["got2"] = x_swap(v["away2"])
    tie("b1", "b7", "b4", "got3", "own3", "own2", "own0", "away0")
    v["d3"], v["d5"] = add((3, 5), v["own3"], v["got3"], SLOW)
    z_back(3, 5)
    v["got0"] = x_swap(v["away0"])
    tie("got2", "own2")
    v["d2"], v["d6"] = add((2, 6), v["own2"], v["got2"])
    z_back(2, 6)
    some, some_dw = pl.pallas_call(
        gather_kernel,
        out_shape=(shape((2, TOKENS, D), F32), shape((2, SLOTS, 1), F32)),
        in_specs=[VMEM] * 8,
        out_specs=(VMEM, VMEM),
        scratch_shapes=[pltpu.VMEM((SLOTS, D), BF16)],
        cost_estimate=pl.CostEstimate(flops=COST, bytes_accessed=1000, transcendentals=0),
        compiler_params=pltpu.CompilerParams(vmem_limit_bytes=LIMIT),
    )(v["own0"], v["got0"], v["b1"], v["b7"], v["b4"], v["b3"], v["b5"], match)
    out = pl.pallas_call(
        finish_kernel,
        out_shape=shape((2, TOKENS, D)),
        in_specs=[VMEM] * 13,
        out_specs=VMEM,
        scratch_shapes=[pltpu.VMEM((2 * CAP + 4 * EXPERTS, D), BF16)],
        cost_estimate=pl.CostEstimate(flops=COST, bytes_accessed=1000, transcendentals=0),
        compiler_params=pltpu.CompilerParams(vmem_limit_bytes=LIMIT),
    )(
        v["b2"],
        v["b6"],
        some,
        some_dw,
        kept,
        saved_in[0],
        routes_t,
        match,
        weight,
        scores,
        inv,
        norm_gain,
        parts,
    )
    return out[None]


def solution(mesh):
    return jax.shard_map(
        local,
        mesh=mesh,
        in_specs=(
            P("pipe", None, "expert", None),
            P("pipe", None, "expert", None),
            P("pipe", None, "expert", None),
            P("pipe", None),
            P("pipe", None, None, None, None, "expert"),
            P("pipe", None, "expert"),
            P("pipe", None, "expert"),
            P("pipe", "expert", None),
            P("pipe", None, None),
            P("pipe", None),
        ),
        out_specs=P("pipe", None, "expert", None),
        check_vma=False,
    )
```

```python
import functools

import jax
import jax.numpy as jnp
from jax import lax
from jax.experimental import pallas as pl
from jax.experimental.pallas import tpu as pltpu
from jax.sharding import PartitionSpec as P

ROUTE_SCALE = 2.5
EPSILON = 1e-06
HIGHEST = lax.Precision.HIGHEST
F32 = jnp.float32
BF16 = jnp.bfloat16
D = 3584
EXPERTS = 8
CAP = 16
TOKENS = 64
SLOTS = EXPERTS * CAP
SLICE = 256
WIDE = D + 128
UNIT = 2 * CAP
NT = (((1,), (1,)), ((), ()))
TN = (((0,), (0,)), ((), ()))
COST = 100_000
SLOW = 20_000_000_000
WORK = 2_000_000_000
LIMIT = 16 * 1024 * 1024

VMEM = pl.BlockSpec(memory_space=pltpu.VMEM)
SMEM = pl.BlockSpec(memory_space=pltpu.SMEM)


def pipe_shift(value, by):
    return lax.ppermute(value, "pipe", [(i, (i + by) % 8) for i in range(8)])


def z_shift(value, by):
    pairs = [(i, ((i // 4 + by) % 8) * 4 + i % 4) for i in range(32)]
    return lax.ppermute(value, "expert", pairs)


def x_swap(value):
    return lax.ppermute(value, "expert", [(i, i ^ 2) for i in range(32)])


def core_swap(value):
    return lax.ppermute(value, "expert", [(i, i ^ 1) for i in range(32)])


def call(kernel, outs, specs, flops, moved):
    return pl.pallas_call(
        kernel,
        out_shape=outs,
        in_specs=specs,
        out_specs=jax.tree.map(lambda _: VMEM, outs),
        cost_estimate=pl.CostEstimate(flops=flops, bytes_accessed=moved, transcendentals=0),
        compiler_params=pltpu.CompilerParams(vmem_limit_bytes=LIMIT),
    )


def lanes(value_hi, value_lo, shape):
    lane = lax.broadcasted_iota(jnp.int32, shape, 1)
    return jnp.where(lane == 0, value_hi, jnp.where(lane == 1, value_lo, 0.0))


def split_sum(tile):
    total = jnp.sum(tile, axis=-1, keepdims=True)
    high = total.astype(BF16).astype(F32)
    return high, total - high


def prep_kernel(
    place, limits, routes, saved, gain, router, match, weight, scores, inv, parts
):
    z = place[0]
    high = router[...].astype(BF16).astype(F32)
    low = router[...] - high
    parts[...] = jnp.concatenate([high, high, low, jnp.zeros_like(low)], axis=0).astype(BF16)
    slot = lax.broadcasted_iota(jnp.int32, (SLOTS, TOKENS), 0)
    expert = ((slot >> 4) + z) & (EXPERTS - 1)
    number = slot & (CAP - 1)
    limit = jnp.zeros((SLOTS, TOKENS), jnp.int32)
    for e in range(EXPERTS):
        limit = jnp.where(expert == e, limits[e], limit)
    allowed = number < limit
    earlier = (
        lax.broadcasted_iota(jnp.int32, (TOKENS, TOKENS), 0)
        < lax.broadcasted_iota(jnp.int32, (TOKENS, TOKENS), 1)
    ).astype(BF16)
    names = lax.broadcasted_iota(jnp.int32, (EXPERTS, TOKENS), 0)
    for m in range(2):
        values = saved[m].astype(F32)
        inv_rms = lax.rsqrt(jnp.mean(values * values, axis=-1, keepdims=True) + EPSILON)
        inv[m] = inv_rms
        normed = values * inv_rms * gain[...]
        logits = lax.dot_general(
            router[...], normed, NT, precision=HIGHEST, preferred_element_type=F32
        )
        score = jax.nn.sigmoid(logits)
        scores[m] = score
        picked = [routes[m, k : k + 1, :] == expert for k in range(2)]
        chosen = [
            jnp.sum(jnp.where(routes[m, k : k + 1, :] == names, score, 0.0), axis=0, keepdims=True)
            for k in range(2)
        ]
        totals = chosen[0] + chosen[1]
        counts = picked[0].astype(F32) + picked[1].astype(F32)
        before = jnp.dot(counts.astype(BF16), earlier, preferred_element_type=F32)
        kept = allowed & (before.astype(jnp.int32) == number)
        column = jnp.zeros((SLOTS, 1), F32)
        for k in range(2):
            hit = (picked[k] & kept).astype(F32)
            match[m, k] = hit
            share = (ROUTE_SCALE * chosen[k] / totals).astype(BF16).astype(F32)
            column = column + jnp.sum(hit * share, axis=-1, keepdims=True)
        weight[m] = column


def split_kernel(sent, first, second, sems):
    copies = [
        pltpu.make_async_copy(sent.at[0, m], out, sems.at[m])
        for m, out in enumerate((first, second))
    ]
    for copy in copies:
        copy.start()
    for copy in copies:
        copy.wait()


def spread_kernel(first, second, match, weight, kept, *outs):
    for m, rows in enumerate((first, second)):
        kept[m] = rows[...]
        both = (match[m, 0] + match[m, 1]).astype(BF16)
        filled = jnp.dot(both, rows[...], preferred_element_type=F32)
        filled = (filled * weight[m]).astype(BF16)
        for k in range(EXPERTS):
            outs[k][m * CAP : (m + 1) * CAP] = filled[k * CAP : (k + 1) * CAP]


def stage_kernel(w_down, w_gate, w_up, packed):
    step = 512
    packed[:SLICE] = w_down[0]
    for at in range(0, D, step):
        packed[SLICE : 2 * SLICE, at : at + step] = w_gate[0, at : at + step].T
        packed[2 * SLICE :, at : at + step] = w_up[0, at : at + step].T


def pack_kernel(low, high, out):
    out[:UNIT] = low[...]
    out[UNIT:] = high[...]


def unit_kernel(shifts, place, mine, theirs, *refs):
    saved, weights = refs[0:2], refs[2:4]
    own, away, rows = refs[4:]
    n = len(shifts)
    z, x = place[0], place[1]
    size = UNIT * 2 * n
    half = size // 2
    rows[:half] = mine[...]
    rows[half:] = theirs[...]
    total = jnp.zeros((size, 1), F32)
    grads = []
    for s in range(2):
        parts = [[], []]
        for side in range(2):
            for shift in shifts:
                source = (z + 8 - shift) & 7
                column = x if side == 0 else 1 - x
                for part in range(2):
                    parts[part].append(saved[s][source, column, part].reshape(UNIT, SLICE))
        gate = jnp.concatenate(parts[0], axis=0).astype(F32)
        up = jnp.concatenate(parts[1], axis=0).astype(F32)
        projected = lax.dot_general(
            rows[...], weights[s][:SLICE], NT, preferred_element_type=F32
        )
        sig = jax.nn.sigmoid(gate)
        act = gate * sig
        total = total + jnp.sum(projected * (act * up), axis=-1, keepdims=True)
        gate_grad = (projected * up * sig * (1.0 + gate * (1.0 - sig))).astype(BF16)
        grads.append(jnp.concatenate([gate_grad, (projected * act).astype(BF16)], axis=1))
    step = 512
    for at in range(0, D, step):
        part = jnp.dot(grads[0], weights[0][SLICE:, at : at + step], preferred_element_type=F32)
        part = part + jnp.dot(
            grads[1], weights[1][SLICE:, at : at + step], preferred_element_type=F32
        )
        own[:, at : at + step] = part[:half]
        away[:, at : at + step] = part[half:].astype(BF16)
    high, low = split_sum(total)
    tile = lanes(high, low, (size, 128))
    own[:, D:] = tile[:half]
    away[:, D:] = tile[half:].astype(BF16)


def add_kernel(own, got, *outs):
    for i, out in enumerate(outs):
        at = slice(i * UNIT, (i + 1) * UNIT)
        out[:, :D] = (own[at, :D] + got[at, :D].astype(F32)).astype(BF16)
        high, low = split_sum(own[at, D:] + got[at, D:].astype(F32))
        out[:, D:] = lanes(high, low, (UNIT, 128)).astype(BF16)


def add_two_kernel(own, got, own_next, got_next, low, high, last):
    add_kernel(own, got, low, high)
    add_kernel(own_next, got_next, last)


def gather_kernel(own, got, b1, b7, b4, b3, b5, match, total, slot_dw, back):
    units = {1: b1, 7: b7, 4: b4, 3: b3, 5: b5}
    for m in range(2):
        at = slice(m * CAP, (m + 1) * CAP)
        back[:CAP] = (own[at, :D] + got[at, :D].astype(F32)).astype(BF16)
        dws = [own[at, D:] + got[at, D:].astype(F32)]
        for k in range(1, EXPERTS):
            rows = slice(k * CAP, (k + 1) * CAP)
            if k in units:
                back[rows] = units[k][at, :D]
                dws.append(units[k][at, D:].astype(F32))
            else:
                back[rows] = jnp.zeros((CAP, D), BF16)
                dws.append(jnp.zeros((CAP, 128), F32))
        slot_dw[m] = jnp.sum(jnp.concatenate(dws, axis=0), axis=-1, keepdims=True)
        both = (match[m, 0] + match[m, 1]).astype(BF16)
        total[m] = lax.dot_general(both, back[...], TN, preferred_element_type=F32)


def finish_kernel(
    b2, b6, some, some_dw, kept, saved, routes, match, weight, scores, inv, gain, parts, out, back
):
    names = lax.broadcasted_iota(jnp.int32, (EXPERTS, TOKENS), 0)
    low, high = slice(2 * CAP, 3 * CAP), slice(6 * CAP, 7 * CAP)
    back[2 * CAP :] = parts[...]
    for m in range(2):
        finish_part(
            m, b2, b6, some, some_dw, kept, saved, routes, match, weight, scores, inv, gain,
            out, back, names, low, high,
        )


def finish_part(
    m, b2, b6, some, some_dw, kept, saved, routes, match, weight, scores, inv, gain, out,
    back, names, low, high,
):
    at = slice(m * CAP, (m + 1) * CAP)
    back[:CAP] = b2[at, :D]
    back[CAP : 2 * CAP] = b6[at, :D]
    late = [jnp.sum(unit[at, D:].astype(F32), axis=-1, keepdims=True) for unit in (b2, b6)]
    slot_dw = some_dw[m]
    slot_dw = jnp.concatenate(
        [slot_dw[: low.start], late[0], slot_dw[low.stop : high.start], late[1], slot_dw[high.stop :]],
        axis=0,
    )
    share = weight[m]
    used = share > 0.0
    slot_dw = jnp.where(used, slot_dw / jnp.where(used, share, 1.0), 0.0)
    score = scores[m]
    chosen, choice, picked = [], [], []
    for k in range(2):
        picked.append(routes[m, k : k + 1, :] == names)
        chosen.append(jnp.sum(jnp.where(picked[k], score, 0.0), axis=0, keepdims=True))
        choice.append(jnp.sum(match[m, k] * slot_dw, axis=0, keepdims=True))
    totals = chosen[0] + chosen[1]
    inner = (choice[0] * chosen[0] + choice[1] * chosen[1]) / (totals * totals)
    score_grad = jnp.zeros((EXPERTS, TOKENS), F32)
    for k in range(2):
        slope = ROUTE_SCALE * (choice[k] / totals - inner)
        score_grad = score_grad + jnp.where(picked[k], slope, 0.0)
    score_grad = score_grad * score * (1.0 - score)
    both = match[m, 0] + match[m, 1]
    main = score_grad.astype(BF16).astype(F32)
    rest = score_grad - main
    both = jnp.concatenate(
        [both[low], both[high], main, rest, main, jnp.zeros_like(main)], axis=0
    ).astype(BF16)
    total = some[m] + lax.dot_general(both, back[...], TN, preferred_element_type=F32)
    scaled = gain[...] * total
    values = saved[m].astype(F32)
    inv_rms = inv[m]
    mean = jnp.mean(values * scaled, axis=-1, keepdims=True)
    out[m] = (
        kept[m].astype(F32)
        + inv_rms * scaled
        - (inv_rms * inv_rms * inv_rms * mean) * values
    ).astype(BF16)


def shape(dims, dtype=BF16):
    return jax.ShapeDtypeStruct(dims, dtype)


def local(
    grads_sent, saved_in, routes, capacity, saved_pre, w_gate, w_up, w_down, router, norm_gain
):
    index = lax.axis_index("expert")
    core = index % 2
    place = jnp.stack([index // 4, (index // 2) % 2]).astype(jnp.int32)
    first, second = pl.pallas_call(
        split_kernel,
        out_shape=(shape((TOKENS, D)), shape((TOKENS, D))),
        in_specs=[pl.BlockSpec(memory_space=pl.ANY)],
        out_specs=(VMEM, VMEM),
        scratch_shapes=[pltpu.SemaphoreType.DMA((2,))],
        cost_estimate=pl.CostEstimate(flops=COST, bytes_accessed=1000, transcendentals=0),
        compiler_params=pltpu.CompilerParams(vmem_limit_bytes=LIMIT),
    )(grads_sent)
    first, second = pipe_shift(first, -1), pipe_shift(second, 1)
    packed = call(stage_kernel, shape((3 * SLICE, D)), [VMEM] * 3, COST, 1000)(
        w_down, w_gate, w_up
    )
    pre = saved_pre[0].reshape(2, 8, 2, 2, CAP, 2, SLICE)
    pre = jnp.transpose(pre, (3, 1, 2, 5, 0, 4, 6))
    routes_t = jnp.transpose(routes[0], (0, 2, 1))
    router_t = router[0].T
    match, weight, scores, inv, parts = call(
        prep_kernel,
        (
            shape((2, 2, SLOTS, TOKENS), F32),
            shape((2, SLOTS, 1), F32),
            shape((2, EXPERTS, TOKENS), F32),
            shape((2, TOKENS, 1), F32),
            shape((4 * EXPERTS, D)),
        ),
        [SMEM, SMEM] + [VMEM] * 4,
        COST,
        1000,
    )(place, capacity[0], routes_t, saved_in[0], norm_gain, router_t)
    pre_own = lax.dynamic_index_in_dim(pre, core, 0, keepdims=False)
    pre_other = lax.dynamic_index_in_dim(pre, 1 - core, 0, keepdims=False)
    first, second, packed, pre_own, pre_other, weight = lax.optimization_barrier(
        (first, second, packed, pre_own, pre_other, weight)
    )
    pre_other, weights = core_swap(pre_other), (packed, core_swap(packed))
    kept, *units = call(
        spread_kernel,
        (shape((2, TOKENS, D)),) + tuple(shape((UNIT, D)) for _ in range(EXPERTS)),
        [VMEM] * 4,
        COST,
        1000,
    )(first, second, match, weight)
    def work(group, mine, theirs, cost=WORK):
        n = len(group)
        return pl.pallas_call(
            functools.partial(unit_kernel, group),
            out_shape=(shape((UNIT * n, WIDE), F32), shape((UNIT * n, WIDE))),
            in_specs=[SMEM] + [VMEM] * 6,
            out_specs=(VMEM, VMEM),
            scratch_shapes=[pltpu.VMEM((2 * UNIT * n, D), BF16)],
            cost_estimate=pl.CostEstimate(flops=cost, bytes_accessed=1000, transcendentals=0),
            compiler_params=pltpu.CompilerParams(vmem_limit_bytes=LIMIT),
        )(place, mine, theirs, pre_own, pre_other, *weights)

    def add(group, own, got, cost=COST):
        return call(add_kernel, tuple(shape((UNIT, WIDE)) for _ in group), [VMEM] * 2, cost, 1000)(
            own, got
        )

    def pack(low, high):
        return call(pack_kernel, shape((2 * UNIT, D)), [VMEM] * 2, COST, 1000)(low, high)

    v = {"u%d" % k: units[k] for k in range(EXPERTS)}

    def tie(*names):
        v.update(zip(names, lax.optimization_barrier(tuple(v[n] for n in names))))

    def z_out(*shifts):
        for k in shifts:
            v["m%d" % k] = z_shift(v["u%d" % k], k)

    def z_back(*shifts):
        for k in shifts:
            v["b%d" % k] = z_shift(v["d%d" % k], -k)

    z_out(1, 7)
    v["t0"] = x_swap(v["u0"])
    tie("m1", "m7", "u4", "u3", "u5", "u2", "u6", "t0", "u0")
    z_out(4)
    v["p1"] = pack(v["m1"], v["m7"])
    v["t1"] = x_swap(v["p1"])
    v["own1"], v["away1"] = work((1, 7), v["p1"], v["t1"])
    v["got1"] = x_swap(v["away1"])
    tie("m4", "own1", "t0", "u0", "u3", "u5", "u2", "u6")
    z_out(3, 5)
    v["t4"] = x_swap(v["m4"])
    v["own4"], v["away4"] = work((4,), v["m4"], v["t4"], SLOW)
    tie("got1", "own1", "own4", "away4", "m3", "m5", "t0", "u0", "u2", "u6")
    z_out(2, 6)
    v["p3"] = pack(v["m3"], v["m5"])
    v["t3"] = x_swap(v["p3"])
    v["got4"] = x_swap(v["away4"])
    v["own3"], v["away3"] = work((3, 5), v["p3"], v["t3"])
    tie("own3", "away3", "m2", "m6", "got4", "own4", "got1", "own1", "t0", "u0")
    v["d1"], v["d7"], v["d4"] = call(
        add_two_kernel, tuple(shape((UNIT, WIDE)) for _ in range(3)), [VMEM] * 4, COST, 1000
    )(v["own1"], v["got1"], v["own4"], v["got4"])
    z_back(1, 7, 4)
    v["p2"] = pack(v["m2"], v["m6"])
    v["t2"] = x_swap(v["p2"])
    v["got3"] = x_swap(v["away3"])
    v["own2"], v["away2"] = work((2, 6), v["p2"], v["t2"])
    v["own0"], v["away0"] = work((0,), v["u0"], v["t0"])
    v["got2"] = x_swap(v["away2"])
    tie("b1", "b7", "b4", "got3", "own3", "own2", "own0", "away0")
    v["d3"], v["d5"] = add((3, 5), v["own3"], v["got3"], SLOW)
    z_back(3, 5)
    v["got0"] = x_swap(v["away0"])
    tie("got2", "own2")
    v["d2"], v["d6"] = add((2, 6), v["own2"], v["got2"])
    z_back(2, 6)
    some, some_dw = pl.pallas_call(
        gather_kernel,
        out_shape=(shape((2, TOKENS, D), F32), shape((2, SLOTS, 1), F32)),
        in_specs=[VMEM] * 8,
        out_specs=(VMEM, VMEM),
        scratch_shapes=[pltpu.VMEM((SLOTS, D), BF16)],
        cost_estimate=pl.CostEstimate(flops=COST, bytes_accessed=1000, transcendentals=0),
        compiler_params=pltpu.CompilerParams(vmem_limit_bytes=LIMIT),
    )(v["own0"], v["got0"], v["b1"], v["b7"], v["b4"], v["b3"], v["b5"], match)
    out = pl.pallas_call(
        finish_kernel,
        out_shape=shape((2, TOKENS, D)),
        in_specs=[VMEM] * 13,
        out_specs=VMEM,
        scratch_shapes=[pltpu.VMEM((2 * CAP + 4 * EXPERTS, D), BF16)],
        cost_estimate=pl.CostEstimate(flops=COST, bytes_accessed=1000, transcendentals=0),
        compiler_params=pltpu.CompilerParams(vmem_limit_bytes=LIMIT),
    )(
        v["b2"],
        v["b6"],
        some,
        some_dw,
        kept,
        saved_in[0],
        routes_t,
        match,
        weight,
        scores,
        inv,
        norm_gain,
        parts,
    )
    return out[None]


def solution(mesh):
    return jax.shard_map(
        local,
        mesh=mesh,
        in_specs=(
            P("pipe", None, "expert", None),
            P("pipe", None, "expert", None),
            P("pipe", None, "expert", None),
            P("pipe", None),
            P("pipe", None, None, None, None, "expert"),
            P("pipe", None, "expert"),
            P("pipe", None, "expert"),
            P("pipe", "expert", None),
            P("pipe", None, None),
            P("pipe", None),
        ),
        out_specs=P("pipe", None, "expert", None),
        check_vma=False,
    )
```
